256 devices in a mesh: seq: 64 (over y, z, core), feat: 4 (over x).
Axes of the slice: x: 4, y: 4, z: 8, core: 2. Of those that a mesh axis runs over, the one named last changes fastest.
Arguments:
- events: bfloat16 [4, 32768, 1024], P('feat', 'seq'), may hold values from -8 to 8
- segment_ids: int32 [4, 32768], P('feat', 'seq'), may hold values from 0 to 15, never falling along the last dimension, each value on 1 to 16384 neighbouring positions
- event_mask: int32 [4, 32768], P('feat', 'seq'), may hold values 0 or 1
- nonseq: bfloat16 [64, 512], P('seq'), may hold values from -6 to 6
- seed_tokens: bfloat16 [16, 1024], replicated, may hold values from -8 to 8
- w_query: bfloat16 [1024, 1024], replicated, may hold values from -1 to 1
- w_key: bfloat16 [1024, 1024], replicated, may hold values from -1 to 1
- w_value: bfloat16 [1024, 1024], replicated, may hold values from -0.1875 to 0.1875
- w_out: bfloat16 [1024, 1024], replicated, may hold values from -0.1875 to 0.1875
- w_pers: bfloat16 [512, 1024], replicated, may hold values from -0.25 to 0.25
- w_comp: bfloat16 [1024, 512], replicated, may hold values from -0.1875 to 0.1875
- w_down: bfloat16 [8192, 128], P('feat'), may hold values from -0.0625 to 0.0625
- w_up: bfloat16 [128, 8192], P(None, 'feat'), may hold values from -0.5 to 0.5
- cross_bias: bfloat16 [8192], P('feat'), may hold values from -3 to 3
Outputs:
- tokens_out: float32 [4, 32768, 1024], P('feat', 'seq')
- cross_out: float32 [64, 8192], P('seq', 'feat')
The draws below stay inside these ranges and needn't reach their ends.
Inputs may be any that keep to these rules, and one draw needn't show every extreme that they name: `segment_ids`: within a group the ids never fall along the events, every id from 0 to 15 occurs, no user has more than 16384 events, and in every draw some user has exactly 16384.
All inputs are finite; a program needn't handle non-finite values. No bound on the sum of `event_mask` on one device may be relied on, other than what follows from the above.
Results may differ from the reference program's by a relative error of at most 0.015.
The reference program's roundings to bfloat16 on the way count: a program that leaves them out, or rounds other values in their place, can miss the bound.
Values may be sent and summed in bfloat16 or wider, within the bound.
No kernel may reach another device: no remote copies, remote signals or barrier semaphores. Data moves between devices by JAX's collectives and lax.ppermute only.
A program may use at most 192 MiB of HBM per device.

```python
import math
import jax
import jax.numpy as jnp
import numpy as np
from jax import lax

D = 1024
HEADS = 8
HEAD_DIM = 128
SEEDS = 16
NSF = 512
SEED_W = 512
CROSS = 8192
RANK = 128
EV_DEV = 512
GROUPS = 4
PACK = 32768
USERS_G = 16
USERS_ALL = 64
MOST = 16384


def key_matrix(key):
    base_draw = jax.random.normal(jax.random.fold_in(key, 800), (D, D), jnp.float32)
    return jnp.clip(base_draw, -6.0, 6.0) * D ** (-0.5)


def draw_events(key, part):
    key = jax.random.fold_in(key, 1)
    key_base = jax.random.fold_in(key, 0)
    values = jnp.clip(jax.random.normal(key_base, (GROUPS, PACK, D), jnp.float32), -8.0, 8.0)
    return values.astype(jnp.bfloat16)


def draw_seed_tokens(key, part):
    key = jax.random.fold_in(key, 2)
    values = jnp.clip(jax.random.normal(key, (SEEDS, D), jnp.float32), -8.0, 8.0)
    return values.astype(jnp.bfloat16)


def draw_w_key(key, part):
    shared = key_matrix(key)
    return shared.astype(jnp.bfloat16)


def draw_w_query(key, part):
    key = jax.random.fold_in(key, 4)
    noise_part = jnp.clip(jax.random.normal(key, (D, D), jnp.float32), -6.0, 6.0) * D ** (-0.5)
    values = noise_part
    return values.astype(jnp.bfloat16)


def touch_ends(result, own_key, least, largest):
    dims = result.shape
    index_at = [jax.random.randint(jax.random.fold_in(own_key, axis), (), 0, dims[axis]) for axis in range(len(dims))]
    result = result.at[tuple(index_at)].set(least)
    longest = dims.index(max(dims))
    index_at[longest] = (index_at[longest] + 1) % dims[longest]
    return result.at[tuple(index_at)].set(largest)


def shard_levels(rng, extent, cuts, least, largest):
    factor_of = 1.0
    for axis_at, blocks in cuts:
        heights = jax.random.uniform(jax.random.fold_in(jax.random.fold_in(rng, 6), axis_at), (blocks,), jnp.float32, least / len(cuts), largest / len(cuts))
        factor_of = factor_of * jnp.repeat(jnp.exp(heights), extent[axis_at] // blocks).reshape((-1,) + (1,) * (len(extent) - 1 - axis_at))
    return factor_of


def length_profile(count, total, most, slope):
    portions = [(1 << 20) // math.isqrt(grade ** slope) + 1 for grade in range(2, count + 1)]
    surplus, holding = total - most - (count - 1), [1] * (count - 1)
    while surplus > 0:
        free = [i for i in range(count - 1) if holding[i] < most]
        whole, remaining = sum([portions[i] for i in free]), surplus
        for i in free:
            addition = min(most - holding[i], max(1, remaining * portions[i] // whole), surplus)
            holding[i] = holding[i] + addition
            surplus = surplus - addition
    return np.array([most] + holding)


def ragged_sizes(stream_key, amount, total, reach, slope):
    if amount == 2:
        one = jax.random.randint(stream_key, (), max(1, total - reach), min(reach, total - 1) + 1)
        return jnp.stack([one, total - one])
    lengths = jnp.asarray(length_profile(amount, total, reach, slope), jnp.int32)
    couples = (amount - 1) // 2
    source_of, receiver = lengths[1:1 + 2 * couples:2], lengths[2:2 + 2 * couples:2]
    slack = jnp.minimum(source_of - 1, reach - receiver)
    moved = jax.random.randint(jax.random.fold_in(stream_key, 1), (couples,), 0, 1 << 20) % (slack + 1)
    lengths = lengths.at[1:1 + 2 * couples:2].set(source_of - moved).at[2:2 + 2 * couples:2].set(receiver + moved)
    return lengths[jax.random.permutation(jax.random.fold_in(stream_key, 2), amount)]


def normal_values(key, dims, deviation, bound, shards=(), held_as=jnp.bfloat16):
    array = jax.random.normal(key, dims, jnp.float32) * deviation
    if len(shards) > 0:
        array = shard_levels(key, dims, shards, -0.22, 0.18) * array
    return jnp.clip(array, min=-bound, max=bound).astype(held_as)


def setup_inputs(seed: int = 0) -> dict:
    arg_keys = jax.random.split(jax.random.key(seed), 15)
    events = draw_events(jax.random.fold_in(arg_keys[14], 71), 0)
    segment_ids = jax.vmap(lambda own: jnp.searchsorted(jnp.cumsum(ragged_sizes(own, USERS_G, PACK, MOST, 2)), jnp.arange(PACK), side="right"))(jax.random.split(arg_keys[1], GROUPS)).reshape((GROUPS, PACK)).astype(jnp.int32)
    event_mask = touch_ends((jax.random.randint(arg_keys[2], (GROUPS, PACK), 0, 8) < 7).astype(jnp.int32), jax.random.fold_in(arg_keys[2], 1), 0, 1)
    nonseq = normal_values(arg_keys[3], (USERS_ALL, NSF), 1.0, 6.0, ((0, 64),))
    seed_tokens = draw_seed_tokens(jax.random.fold_in(arg_keys[14], 71), 0)
    w_query = draw_w_query(jax.random.fold_in(arg_keys[14], 71), 0)
    w_key = draw_w_key(jax.random.fold_in(arg_keys[14], 71), 0)
    w_value = normal_values(arg_keys[7], (D, D), D ** -0.5, 0.1875)
    w_out = normal_values(arg_keys[8], (D, D), D ** -0.5, 0.1875)
    w_pers = normal_values(arg_keys[9], (NSF, D), NSF ** -0.5, 0.25)
    w_comp = normal_values(arg_keys[10], (D, SEED_W), D ** -0.5, 0.1875)
    w_down = normal_values(arg_keys[11], (CROSS, RANK), CROSS ** -0.5, 0.0625, ((0, 4),))
    w_up = normal_values(arg_keys[12], (RANK, CROSS), RANK ** -0.5, 0.5, ((1, 4),))
    cross_bias = normal_values(arg_keys[13], (CROSS,), 0.5, 3.0, ((0, 4),))
    return dict(events=events, segment_ids=segment_ids, event_mask=event_mask, nonseq=nonseq, seed_tokens=seed_tokens, w_query=w_query, w_key=w_key, w_value=w_value, w_out=w_out, w_pers=w_pers, w_comp=w_comp, w_down=w_down, w_up=w_up, cross_bias=cross_bias)


HIGHEST = lax.Precision.HIGHEST
NEGATIVE = -1e+30

def attend_group(tokens, segments, kept_flags, w_query, w_key, w_value, w_out):
    score_scale = HEAD_DIM ** (-0.5)
    queries = jnp.dot(tokens, w_query, preferred_element_type=jnp.float32).astype(jnp.bfloat16)
    key_rows = jnp.dot(tokens, w_key, preferred_element_type=jnp.float32).astype(jnp.bfloat16)
    value_rows = jnp.dot(tokens, w_value, preferred_element_type=jnp.float32).astype(jnp.bfloat16)
    pad_rows = jnp.zeros((EV_DEV, D), jnp.bfloat16)
    keys_pad = jnp.concatenate([pad_rows, key_rows], 0)
    values_pad = jnp.concatenate([pad_rows, value_rows], 0)
    segments_pad = jnp.concatenate([jnp.full((EV_DEV,), -1, jnp.int32), segments], 0)
    flags_pad = jnp.concatenate([jnp.zeros((EV_DEV,), jnp.int32), kept_flags], 0)
    query_pos = jnp.arange(EV_DEV, dtype=jnp.int32)[:, None]
    key_pos = jnp.arange(2 * EV_DEV, dtype=jnp.int32)[None, :]
    in_window = (key_pos > query_pos) & (key_pos <= query_pos + EV_DEV)
    itself = key_pos == query_pos + EV_DEV

    def one_block(block_index):
        row_start = (block_index * EV_DEV).astype(jnp.int32)
        query_block = lax.dynamic_slice_in_dim(queries, row_start, EV_DEV, 0).astype(jnp.float32).reshape(EV_DEV, HEADS, HEAD_DIM)
        key_block = lax.dynamic_slice_in_dim(keys_pad, row_start, 2 * EV_DEV, 0).astype(jnp.float32).reshape(2 * EV_DEV, HEADS, HEAD_DIM)
        value_block = lax.dynamic_slice_in_dim(values_pad, row_start, 2 * EV_DEV, 0).astype(jnp.float32).reshape(2 * EV_DEV, HEADS, HEAD_DIM)
        query_segments = lax.dynamic_slice_in_dim(segments, row_start, EV_DEV, 0)
        key_segments = lax.dynamic_slice_in_dim(segments_pad, row_start, 2 * EV_DEV, 0)
        key_flags = lax.dynamic_slice_in_dim(flags_pad, row_start, 2 * EV_DEV, 0)
        allowed = (query_segments[:, None] == key_segments[None, :]) & in_window & ((key_flags[None, :] == 1) | itself)
        scores = jnp.einsum('qhd,khd->hqk', query_block, key_block) * score_scale
        masked = jnp.where(allowed[None], scores, NEGATIVE)
        row_top = lax.optimization_barrier(jnp.max(masked, -1, keepdims=True))
        weights = jnp.exp(masked - row_top)
        row_total = lax.optimization_barrier(jnp.sum(weights, -1))
        rounded = lax.optimization_barrier(weights.astype(jnp.bfloat16)).astype(jnp.float32)
        mixed_sum = jnp.einsum('hqk,khd->qhd', rounded, value_block)
        return (mixed_sum / jnp.transpose(row_total)[:, :, None]).astype(jnp.bfloat16).reshape(EV_DEV, D)
    context = lax.map(one_block, jnp.arange(PACK // EV_DEV, dtype=jnp.int32)).reshape(PACK, D)
    full_out = tokens.astype(jnp.float32) + jnp.dot(context, w_out, preferred_element_type=jnp.float32)
    hidden = lax.optimization_barrier(full_out.astype(jnp.bfloat16))
    return (full_out, hidden, key_rows)

def pool_group(hidden, key_rows, segments, kept_flags, seed_query, group_query):
    score_scale = HEAD_DIM ** (-0.5)
    previous = jnp.concatenate([jnp.full((1,), -1, jnp.int32), segments[:-1]], 0)
    usable = (kept_flags == 1) | (segments != previous)
    key_heads = key_rows.astype(jnp.float32).reshape(PACK, HEADS, HEAD_DIM)
    seed_heads = seed_query.astype(jnp.float32).reshape(SEEDS, HEADS, HEAD_DIM)
    event_query = group_query[segments].astype(jnp.float32).reshape(PACK, HEADS, HEAD_DIM)
    pool_score = (jnp.einsum('ehd,shd->esh', key_heads, seed_heads) + jnp.einsum('ehd,ehd->eh', key_heads, event_query)[:, None, :]) * score_scale
    flat_score = pool_score.reshape(PACK, SEEDS * HEADS)

    def peak_of(user_id):
        member = (segments == user_id) & usable
        return lax.optimization_barrier(jnp.max(jnp.where(member[:, None], flat_score, NEGATIVE), 0))
    user_peak = lax.map(peak_of, jnp.arange(USERS_G, dtype=jnp.int32))
    weights = jnp.where(usable[:, None], jnp.exp(flat_score - user_peak[segments]), 0.0)
    onehot = (segments[:, None] == jnp.arange(USERS_G, dtype=jnp.int32)[None, :]).astype(jnp.float32)
    totals = jnp.dot(jnp.transpose(onehot), weights, precision=HIGHEST)
    rounded = lax.optimization_barrier(weights.astype(jnp.bfloat16)).astype(jnp.float32)
    weight_grid = rounded.reshape(PACK, SEEDS, HEADS)
    head_parts = []
    for head_index in range(HEADS):
        spread = (onehot[:, :, None] * weight_grid[:, None, :, head_index]).reshape(PACK, USERS_G * SEEDS)
        features = hidden[:, head_index * HEAD_DIM:(head_index + 1) * HEAD_DIM].astype(jnp.float32)
        head_parts.append(jnp.dot(jnp.transpose(spread), features, precision=HIGHEST))
    weighted = jnp.stack(head_parts, 1).reshape(USERS_G, SEEDS, HEADS, HEAD_DIM)
    pooled = (weighted / totals.reshape(USERS_G, SEEDS, HEADS)[:, :, :, None]).reshape(USERS_G, SEEDS, D)
    return (pooled * lax.rsqrt(lax.optimization_barrier(jnp.mean(pooled * pooled, -1, keepdims=True)) + 1e-06)).astype(jnp.bfloat16)

def reference(events, segment_ids, event_mask, nonseq, seed_tokens, w_query, w_key, w_value, w_out, w_pers, w_comp, w_down, w_up, cross_bias):
    profile = jnp.dot(nonseq, w_pers, preferred_element_type=jnp.float32).astype(jnp.bfloat16)
    user_query = jnp.dot(profile, w_query, preferred_element_type=jnp.float32).astype(jnp.bfloat16)
    seed_query = jnp.dot(seed_tokens, w_query, preferred_element_type=jnp.float32).astype(jnp.bfloat16)
    token_list = []
    summaries = []
    for group_index in range(GROUPS):
        full_out, hidden, key_rows = attend_group(events[group_index], segment_ids[group_index], event_mask[group_index], w_query, w_key, w_value, w_out)
        token_list.append(full_out)
        group_query = user_query[group_index * USERS_G:(group_index + 1) * USERS_G]
        summaries.append(pool_group(hidden, key_rows, segment_ids[group_index], event_mask[group_index], seed_query, group_query))
    tokens_out = jnp.stack(token_list, 0)
    summary = jnp.concatenate(summaries, 0)
    context_row = jnp.dot(summary.reshape(USERS_ALL * SEEDS, D), w_comp, preferred_element_type=jnp.float32).astype(jnp.bfloat16).reshape(USERS_ALL, CROSS)
    rank_part = jnp.dot(context_row, w_down, preferred_element_type=jnp.float32).astype(jnp.bfloat16)
    lifted = jnp.dot(rank_part, w_up, preferred_element_type=jnp.float32)
    base_row = context_row.astype(jnp.float32)
    cross_out = base_row * (lifted + cross_bias.astype(jnp.float32)[None, :]) + base_row
    return (tokens_out, cross_out)
```

```python
import functools
import jax
import jax.numpy as jnp
from jax import lax
from jax.experimental import pallas as pl
from jax.experimental.pallas import tpu as pltpu
from jax.sharding import Mesh, PartitionSpec as P

HEADS = 8
HEAD_DIM = 128
SEEDS = 16
USERS = 16
ROWS = 512
WIDTH = 1024
CHUNK = 256
PAIR = 256
EXTRA = 128
MESSAGE = WIDTH + EXTRA
NEGATIVE = -1e30
ABSENT = -1e29
LOG2E = 1.4426950408889634
SCALE = HEAD_DIM**-0.5 * LOG2E
F32 = jnp.float32
BF16 = jnp.bfloat16


def dot(a, b):
    return jnp.dot(a, b, preferred_element_type=F32)


def dot_rows(a, b):
    return lax.dot_general(a, b, (((1,), (1,)), ((), ())), preferred_element_type=F32)


def same_user(query_segments, key_segments, key_flags):
    ids = lax.broadcasted_iota(jnp.int32, (USERS, ROWS), 0)
    left = jnp.where(query_segments == ids, 1.0, 0.0).astype(BF16)
    right = jnp.where((key_segments == ids) & (key_flags == 1), 1.0, 0.0).astype(BF16)
    match = lax.dot_general(left, right, (((0,), (0,)), ((), ())), preferred_element_type=F32)
    return match > 0.5


def own_body(x_ref, seg_ref, flag_ref, wq_ref, wk_ref, wv_ref, q_ref, k_ref, acc_ref, ml_ref, bias_ref):
    @pl.when(pl.program_id(0) == 0)
    def _():
        row = lax.broadcasted_iota(jnp.int32, (ROWS, ROWS), 0)
        col = lax.broadcasted_iota(jnp.int32, (ROWS, ROWS), 1)
        same = same_user(seg_ref[...], seg_ref[...], flag_ref[...])
        bias_ref[...] = jnp.where((same & (col < row)) | (col == row), 0.0, NEGATIVE)

    x = x_ref[...]
    q = dot(x, wq_ref[...]).astype(BF16)
    k = dot(x, wk_ref[...]).astype(BF16)
    v = dot(x, wv_ref[...]).astype(BF16)
    q_ref[...] = q
    k_ref[...] = k
    lane = lax.broadcasted_iota(jnp.int32, (CHUNK, 128), 1)
    for at in range(0, ROWS, CHUNK):
        end = at + CHUNK
        stats = jnp.zeros((CHUNK, 128), F32)
        for half in range(PAIR // HEAD_DIM):
            cols = slice(half * HEAD_DIM, (half + 1) * HEAD_DIM)
            score = dot_rows(q[at:end, cols], k[:end, cols]) * SCALE + bias_ref[at:end, :end]
            top = jnp.max(score, 1, keepdims=True)
            weight = jnp.exp2(score - top)
            total = jnp.sum(weight, 1, keepdims=True)
            acc_ref[at:end, cols] = dot(weight.astype(BF16), v[:end, cols])
            stats = jnp.where(lane == half, top, jnp.where(lane == half + 2, total, stats))
        ml_ref[0, at:end, :] = stats


def prior_body(
    xp_ref, x_ref, seg_ref, segp_ref, flagp_ref, wk_ref, wv_ref, wo_ref, q_ref, acc_ref, ml_ref,
    out_ref, hid_ref, bias_ref,
):
    step = pl.program_id(0)

    @pl.when(step == 0)
    def _():
        row = lax.broadcasted_iota(jnp.int32, (ROWS, ROWS), 0)
        col = lax.broadcasted_iota(jnp.int32, (ROWS, ROWS), 1)
        same = same_user(seg_ref[...], segp_ref[...], flagp_ref[...])
        bias_ref[...] = jnp.where(same & (col > row), 0.0, NEGATIVE)
        out_ref[...] = x_ref[...].astype(F32)

    xp = xp_ref[...]
    k = dot(xp, wk_ref[...]).astype(BF16)
    v = dot(xp, wv_ref[...]).astype(BF16)
    for at in range(0, ROWS, CHUNK):
        end = at + CHUNK
        parts = []
        for half in range(PAIR // HEAD_DIM):
            cols = slice(half * HEAD_DIM, (half + 1) * HEAD_DIM)
            score = dot_rows(q_ref[at:end, cols], k[at:, cols]) * SCALE + bias_ref[at:end, at:]
            before = ml_ref[0, at:end, half : half + 1]
            total = ml_ref[0, at:end, half + 2 : half + 3]
            top = jnp.maximum(before, jnp.max(score, 1, keepdims=True))
            weight = jnp.exp2(score - top)
            shrink = jnp.exp2(before - top)
            total = total * shrink + jnp.sum(weight, 1, keepdims=True)
            mixed = acc_ref[at:end, cols] * shrink + dot(weight.astype(BF16), v[at:, cols])
            parts.append((mixed / total).astype(BF16))
        out_ref[at:end, :] += dot(jnp.concatenate(parts, 1), wo_ref[...])

    @pl.when(step == pl.num_programs(0) - 1)
    def _():
        hid_ref[...] = out_ref[...].astype(BF16)


def split_terms(stats, lane):
    high = stats.astype(BF16).astype(F32)
    rest = stats - high
    middle = rest.astype(BF16).astype(F32)
    low = rest - middle
    return jnp.where(lane < 16, high, jnp.where(lane < 32, middle, low)).astype(BF16)


def join_terms(extra):
    extra = extra.astype(F32)
    return extra + pltpu.roll(extra, 112, 1) + pltpu.roll(extra, 96, 1)


def pool_body(place_ref, hid_ref, k_ref, sq_ref, uq_ref, seg_ref, segp_ref, flag_ref, keep_ref, send_ref):
    core = place_ref[0]
    own_user = place_ref[1]
    count = USERS * SEEDS
    row = lax.broadcasted_iota(jnp.int32, (count, 16), 0)
    col = lax.broadcasted_iota(jnp.int32, (count, 16), 1)
    user16 = ((row % 32) // 4) * 2 + (core ^ (row // 128))
    seed16 = ((row % 128) // 32) * 4 + row % 4
    pick_seed = jnp.where(col == seed16, 1.0, 0.0).astype(BF16)
    pick_user = jnp.where(col == (user16 ^ own_user), 1.0, 0.0).astype(BF16)
    seeds = dot(pick_seed, sq_ref[...]).astype(BF16)
    users = dot(pick_user, uq_ref[...]).astype(BF16)

    segs = seg_ref[...]
    lanes = lax.broadcasted_iota(jnp.int32, (8, ROWS), 1)
    before = pltpu.roll(jnp.broadcast_to(segs, (8, ROWS)), 1, 1)
    before = jnp.where(lanes == 0, segp_ref[:, ROWS - 1 :], before)
    usable = (flag_ref[...] == 1) | (segs != before[0:1])
    marked = jnp.where(usable, segs, -1)
    wide = lax.broadcasted_iota(jnp.int32, (count, ROWS), 0)
    user_of = ((wide % 32) // 4) * 2 + (core ^ (wide // 128))
    bias = jnp.where(marked == user_of, 0.0, NEGATIVE)

    lane = lax.broadcasted_iota(jnp.int32, (count, 128), 1)
    stats = jnp.zeros((count, 128), F32)
    for head in range(HEADS):
        cols = slice(head * HEAD_DIM, (head + 1) * HEAD_DIM)
        keys = k_ref[:, cols]
        queries = jnp.concatenate([seeds[:, cols], users[:, cols]], 1)
        score = dot_rows(queries, jnp.concatenate([keys, keys], 1)) * SCALE + bias
        top = jnp.maximum(jnp.max(score, 1, keepdims=True), ABSENT)
        weight = jnp.exp2(score - top)
        total = jnp.sum(weight, 1, keepdims=True)
        pooled = dot(weight.astype(BF16), hid_ref[:, cols]).astype(BF16)
        keep_ref[:, cols] = pooled[:128]
        send_ref[:, cols] = pooled[128:]
        place = lane % 16
        stats = jnp.where(place == head, top, jnp.where(place == head + 8, total, stats))
    extra = jnp.where(lane < 48, split_terms(stats, lane), jnp.zeros((), BF16))
    keep_ref[:, WIDTH:] = extra[:128]
    send_ref[:, WIDTH:] = extra[128:]


def merge_body(a_ref, b_ref, out_ref):
    a = join_terms(a_ref[:, WIDTH:])
    b = join_terms(b_ref[:, WIDTH:])
    top = jnp.maximum(a, b)
    scale_a = jnp.exp2(a - top)
    scale_b = jnp.exp2(b - top)
    lane = lax.broadcasted_iota(jnp.int32, a.shape, 1)
    total = a * pltpu.roll(scale_a, 8, 1) + b * pltpu.roll(scale_b, 8, 1)
    stats = jnp.where(lane < 8, top, jnp.where(lane < 16, total, 0.0))
    stats = stats + pltpu.roll(stats, 16, 1) + pltpu.roll(stats, 32, 1)
    out_ref[:, WIDTH:] = jnp.where(lane < 48, split_terms(stats, lane), jnp.zeros((), BF16))
    for head in range(HEADS):
        cols = slice(head * HEAD_DIM, (head + 1) * HEAD_DIM)
        out_ref[:, cols] = (
            a_ref[:, cols].astype(F32) * scale_a[:, head : head + 1]
            + b_ref[:, cols].astype(F32) * scale_b[:, head : head + 1]
        ).astype(BF16)


def finish_body(in_ref, comp_ref, down_ref, row_ref, rank_ref):
    stats = join_terms(in_ref[:, WIDTH:]).reshape(16, 8, 128)
    top = jnp.max(stats, 0)
    top = jnp.maximum(top, pltpu.roll(top, 4, 0))
    scale = jnp.exp2(stats - top[None])
    shifted = pltpu.roll(scale.reshape(128, 128), 8, 1).reshape(16, 8, 128)
    total = jnp.sum(stats * shifted, 0)
    total = total + pltpu.roll(total, 4, 0)
    parts = []
    for head in range(HEADS):
        cols = slice(head * HEAD_DIM, (head + 1) * HEAD_DIM)
        data = in_ref[:, cols].astype(F32).reshape(16, 8, 128)
        part = jnp.sum(data * scale[:, :, head : head + 1], 0)
        part = part + pltpu.roll(part, 4, 0)
        parts.append(part / total[:, head + 8 : head + 9])
    pooled = jnp.concatenate(parts, 1)
    mean = jnp.mean(pooled * pooled, 1, keepdims=True)
    summary = (pooled * lax.rsqrt(mean + 1e-06)).astype(BF16)
    context = dot(summary, comp_ref[...]).astype(BF16)
    rank = jnp.zeros((1, 128), F32)
    for seed in range(4):
        rank = rank + dot(context, down_ref[seed * 512 : (seed + 1) * 512, :])[seed : seed + 1]
    wide = lax.broadcasted_iota(jnp.int32, (8, 512), 0)
    spread = jnp.concatenate([rank] + [jnp.zeros((1, 128), F32)] * 3, 1)
    row_ref[...] = jnp.where(wide < 4, context.astype(F32), spread)
    rank_ref[...] = jnp.broadcast_to(rank, (8, 128))


def cross_body(row_ref, b_ref, c_ref, d_ref, up_ref, bias_ref, out_ref):
    rank = row_ref[4:5, :128] + b_ref[0:1] + c_ref[0:1] + d_ref[0:1]
    rank = jnp.broadcast_to(rank, (8, 128)).astype(BF16)
    lifted = dot(rank, up_ref[...])[0:1]
    base = jnp.concatenate([row_ref[seed : seed + 1, :] for seed in range(4)], 1)
    out_ref[...] = base * (lifted + bias_ref[...].astype(F32)) + base


def shape(dims, dtype):
    return jax.ShapeDtypeStruct(dims, dtype)


def whole():
    return pl.BlockSpec(memory_space=pltpu.VMEM)


def cost(flops, nbytes, exps=0):
    return pl.CostEstimate(flops=flops, bytes_accessed=nbytes, transcendentals=exps)


def params(megabytes):
    return pltpu.CompilerParams(vmem_limit_bytes=megabytes << 20)


def attend_own(x, segs, flags, w_query, w_key, w_value):
    fixed = lambda dims: pl.BlockSpec(dims, lambda i: (0,) * len(dims))
    cols = lambda rows: pl.BlockSpec((rows, PAIR), lambda i: (0, i))
    steps = WIDTH // PAIR
    return pl.pallas_call(
        own_body,
        grid=(steps,),
        in_specs=[fixed((ROWS, WIDTH)), fixed((1, ROWS)), fixed((1, ROWS))] + [cols(WIDTH)] * 3,
        out_specs=[cols(ROWS)] * 3 + [pl.BlockSpec((1, ROWS, 128), lambda i: (i, 0, 0))],
        out_shape=[
            shape((ROWS, WIDTH), BF16),
            shape((ROWS, WIDTH), BF16),
            shape((ROWS, WIDTH), F32),
            shape((steps, ROWS, 128), F32),
        ],
        scratch_shapes=[pltpu.VMEM((ROWS, ROWS), F32)],
        compiler_params=params(32),
        cost_estimate=cost(5 << 30, 12 << 20, 2 << 20),
        name="own",
    )(x, segs, flags, w_query, w_key, w_value)


def attend_prior(xp, x, segs, segp, flagp, w_key, w_value, w_out, q, acc, ml):
    fixed = lambda dims: pl.BlockSpec(dims, lambda i: (0,) * len(dims))
    cols = lambda rows: pl.BlockSpec((rows, PAIR), lambda i: (0, i))
    steps = WIDTH // PAIR
    return pl.pallas_call(
        prior_body,
        grid=(steps,),
        in_specs=[fixed((ROWS, WIDTH))] * 2
        + [fixed((1, ROWS))] * 3
        + [cols(WIDTH)] * 2
        + [pl.BlockSpec((PAIR, WIDTH), lambda i: (i, 0)), cols(ROWS), cols(ROWS)]
        + [pl.BlockSpec((1, ROWS, 128), lambda i: (i, 0, 0))],
        out_specs=[fixed((ROWS, WIDTH))] * 2,
        out_shape=[shape((ROWS, WIDTH), F32), shape((ROWS, WIDTH), BF16)],
        scratch_shapes=[pltpu.VMEM((ROWS, ROWS), F32)],
        compiler_params=params(40),
        cost_estimate=cost(5 << 30, 14 << 20, 2 << 20),
        name="prior",
    )(xp, x, segs, segp, flagp, w_key, w_value, w_out, q, acc, ml)


def call(body, outs, args, specs=None, flops=1 << 28, nbytes=2 << 20, name=None):
    return pl.pallas_call(
        body,
        in_specs=specs or [whole()] * len(args),
        out_specs=[whole()] * len(outs),
        out_shape=outs,
        compiler_params=params(24),
        cost_estimate=cost(flops, nbytes),
        name=name,
    )(*args)


def swap(value, turn=0):
    pairs = [(q * 4 + g, g * 4 + (q + turn) % 4) for q in range(4) for g in range(4)]
    return lax.ppermute(value, ("y", "x"), pairs)


def flip(value, axis, size, bit):
    return lax.ppermute(value, axis, [(i, i ^ bit) for i in range(size)])


def local(
    events, segment_ids, event_mask, nonseq, seed_tokens, w_query, w_key, w_value, w_out, w_pers,
    w_comp, w_down, w_up, cross_bias,
):
    x = events[0]
    first = (lax.axis_index("y") == 0) & (lax.axis_index("z") == 0) & (lax.axis_index("core") == 0)
    core = lax.axis_index("core").astype(jnp.int32)
    own_user = lax.axis_index("z").astype(jnp.int32) * 2 + core
    line = ("y", "z", "core")
    onward = [(i, i + 1) for i in range(63)]
    xp = lax.ppermute(x, line, onward)
    marks = lax.ppermute(jnp.concatenate([segment_ids, event_mask], 0), line, onward)
    segp = jnp.where(first, -1, marks[0:1])
    flagp = marks[1:2]

    users = swap(nonseq)
    users = jnp.concatenate([users, flip(users, "core", 2, 1)], 0)
    for bit in (1, 2, 4):
        users = jnp.concatenate([users, flip(users, "z", 8, bit)], 0)
    down = swap(w_down)

    q, k, acc, ml = attend_own(x, segment_ids, event_mask, w_query, w_key, w_value)
    profile = dot(users, w_pers).astype(BF16)
    user_query = dot(profile, w_query).astype(BF16)
    seed_query = dot(seed_tokens, w_query).astype(BF16)
    out, hidden = attend_prior(
        xp, x, segment_ids, segp, flagp, w_key, w_value, w_out, q, acc, ml
    )
    half = shape((128, MESSAGE), BF16)
    keep, send = call(
        pool_body,
        [half, half],
        [jnp.stack([core, own_user]), hidden, k, seed_query, user_query, segment_ids, segp, event_mask],
        [pl.BlockSpec(memory_space=pltpu.SMEM)] + [whole()] * 7,
        name="pool",
    )
    received = flip(send, "core", 2, 1)
    merged = call(merge_body, [half], [keep, received], name="merge")[0]
    pieces = lax.all_to_all(merged.reshape(32, 4, MESSAGE), ("y", "z"), 0, 0, tiled=True)
    row, rank = call(
        finish_body,
        [shape((8, 512), F32), shape((8, 128), F32)],
        [pieces.reshape(128, MESSAGE), w_comp, down],
        name="finish",
    )
    row = swap(row)
    ranks = [swap(rank, turn) for turn in (1, 2, 3)]
    cross = call(
        cross_body,
        [shape((1, 2048), F32)],
        [row] + ranks + [w_up, cross_bias[None]],
        name="cross",
    )[0]
    return out[None], cross


def solution(mesh):
    split = Mesh(mesh.devices.reshape(4, 8, 2, 4), ("y", "z", "core", "x"))
    seq = ("y", "z", "core")
    return jax.shard_map(
        local,
        mesh=split,
        in_specs=(
            P("x", seq, None), P("x", seq), P("x", seq), P(seq, None),
            P(), P(), P(), P(), P(), P(), P(),
            P("x", None), P(None, "x"), P("x"),
        ),
        out_specs=(P("x", seq, None), P(seq, "x")),
        check_vma=False,
    )
```

```python
import functools
import jax
import jax.numpy as jnp
from jax import lax
from jax.experimental import pallas as pl
from jax.experimental.pallas import tpu as pltpu
from jax.sharding import Mesh, PartitionSpec as P

HEADS = 8
HEAD_DIM = 128
SEEDS = 16
USERS = 16
ROWS = 512
WIDTH = 1024
HALF = 256
CHUNK = 256
PIECE = 512
EXTRA = 128
MESSAGE = WIDTH + EXTRA
SPAN = WIDTH // 2
NEGATIVE = -1e30
ABSENT = -1e29
LOG2E = 1.4426950408889634
SCALE = HEAD_DIM**-0.5 * LOG2E
F32 = jnp.float32
BF16 = jnp.bfloat16


def dot(a, b):
    return jnp.dot(a, b, preferred_element_type=F32)


def dot_rows(a, b):
    return lax.dot_general(a, b, (((1,), (1,)), ((), ())), preferred_element_type=F32)


def same_user(query_segments, key_segments, key_flags):
    def users(ids, kept):
        ones = (ids == lax.broadcasted_iota(jnp.int32, (USERS, ids.shape[1]), 0)) & kept
        return jnp.where(ones, 1.0, 0.0).astype(BF16)

    left = users(query_segments, True)
    right = users(key_segments, key_flags == 1)
    match = lax.dot_general(left, right, (((0,), (0,)), ((), ())), preferred_element_type=F32)
    return match > 0.5


def square(rows, cols):
    row = lax.broadcasted_iota(jnp.int32, (rows, cols), 0)
    return row, lax.broadcasted_iota(jnp.int32, (rows, cols), 1)


def head_cols(head):
    return slice(head * HEAD_DIM, (head + 1) * HEAD_DIM)


def beside_ones(values):
    return jnp.concatenate([values, jnp.ones(values.shape, BF16)], 1)


def load_body(x_hbm, seg_hbm, flag_hbm, high_ref, low_ref, seg_ref, flag_ref, sems):
    quarter = HALF // 2
    copies = [
        pltpu.make_async_copy(seg_hbm, seg_ref, sems.at[0]),
        pltpu.make_async_copy(flag_hbm, flag_ref, sems.at[1]),
    ]
    for start, target in ((HALF, high_ref), (0, low_ref)):
        for at in (0, quarter):
            copies.append(
                pltpu.make_async_copy(
                    x_hbm.at[pl.ds(start + at, quarter)], target.at[pl.ds(at, quarter)], sems.at[len(copies)]
                )
            )
    for copy in copies:
        copy.start()
    copies[0].wait()
    copies[1].wait()
    row, _ = square(16, ROWS)
    marks = jnp.where(row == 0, seg_ref[...], jnp.where(row == 1, flag_ref[...], 0))
    high_ref[HALF:, :ROWS] = marks.astype(F32).astype(BF16)
    high_ref[HALF:, ROWS:] = jnp.zeros((16, WIDTH - ROWS), BF16)
    for copy in copies[2:]:
        copy.wait()


def project_body(
    place_ref, low_ref, high_ref, wq_hbm, wk_hbm, wv_hbm, wo_hbm, seg_ref, flag_ref,
    wq_ref, wk_ref, wv_ref, wo_ref, q_ref, k_ref, v_ref, bias_ref, sems,
):
    copies = []
    triples = [(wq_hbm, wq_ref, q_ref), (wk_hbm, wk_ref, k_ref), (wv_hbm, wv_ref, v_ref)]
    for source, target, _ in triples:
        for at in range(0, WIDTH, PIECE):
            cols = slice(at, at + PIECE)
            copies.append(
                pltpu.make_async_copy(source.at[:, cols], target.at[:, cols], sems.at[len(copies)])
            )
    copies.append(pltpu.make_async_copy(wo_hbm, wo_ref, sems.at[len(copies)]))
    for copy in copies:
        copy.start()
    row, col = square(ROWS, ROWS)
    same = same_user(seg_ref[...], seg_ref[...], flag_ref[...])
    bias_ref[...] = jnp.where((same & (col < row)) | (col == row), 0.0, NEGATIVE)
    x = jnp.concatenate([low_ref[...], high_ref[:HALF]], 0)
    at = 0
    for _, weight, result in triples:
        for start in range(0, WIDTH, PIECE):
            cols = slice(start, start + PIECE)
            copies[at].wait()
            result[:, cols] = dot(x, weight[:, cols]).astype(BF16)
            at += 1
    copies[at].wait()


def query_body(a_ref, b_ref, c_ref, d_ref, e_ref, pers_ref, wq_ref, seed_ref, sq_ref, uq_ref):
    rows = [ref[...].astype(F32) for ref in (a_ref, b_ref, c_ref, d_ref, e_ref)]
    profile = dot(jnp.concatenate(rows, 0).astype(BF16), pers_ref[...])
    both = jnp.concatenate([seed_ref[...].astype(F32), profile], 0).astype(BF16)
    queries = dot(both, wq_ref[...]).astype(BF16)
    sq_ref[...] = queries[:SEEDS]
    uq_ref[...] = queries[SEEDS:]


def own_body(q_ref, k_ref, v_ref, bias_ref, acc_ref, top_ref, total_ref):
    for head in range(HEADS):
        cols = head_cols(head)
        values = beside_ones(v_ref[:, cols])
        for at in range(0, ROWS, CHUNK):
            end = at + CHUNK
            score = dot_rows(q_ref[at:end, cols], k_ref[:end, cols]) * SCALE + bias_ref[at:end, :end]
            top = jnp.max(score, 1, keepdims=True)
            mixed = dot(jnp.exp2(score - top).astype(BF16), values[:end])
            acc_ref[at:end, cols] = mixed[:, :HEAD_DIM]
            total_ref[at:end, cols] = mixed[:, HEAD_DIM:]
            top_ref[at:end, cols] = jnp.broadcast_to(top, (CHUNK, HEAD_DIM))


def absorb(queries, keys, values, bias, mixed, top, total):
    score = dot_rows(queries, keys) * SCALE + bias
    before = top
    top = jnp.maximum(before, jnp.max(score, 1, keepdims=True))
    weights = [
        jnp.exp2(score[:, at : at + HEAD_DIM] - top) for at in range(0, score.shape[1], HEAD_DIM)
    ]
    fresh = dot(jnp.concatenate(weights, 1).astype(BF16), values)
    shrink = jnp.exp2(before - top)
    return mixed * shrink + fresh[:, :HEAD_DIM], top, total * shrink + fresh[:, HEAD_DIM:]


def marks_of(place_ref, near_ref, cols):
    marks = near_ref[HALF:, cols].astype(F32).astype(jnp.int32)
    return jnp.where(place_ref[2] == 1, -1, marks[0:1]), marks[1:2]


def near_body(
    place_ref, xp_ref, wk_ref, wv_ref, wo_ref, x_ref, q_ref, acc_ref, top_ref, total_ref, seg_ref,
    out_ref, hid_ref, acc2_ref, top2_ref, total2_ref, bias_ref, key_ref, value_ref, context_ref,
):
    segp, flagp = marks_of(place_ref, xp_ref, slice(HALF, ROWS))
    row, col = square(ROWS, HALF)
    same = same_user(seg_ref[...], segp, flagp)
    bias_ref[...] = jnp.where(same & (col + HALF > row), 0.0, NEGATIVE)
    xp = xp_ref[:HALF]
    key_ref[...] = dot(xp, wk_ref[...]).astype(BF16)
    value_ref[...] = dot(xp, wv_ref[...]).astype(BF16)
    for head in range(HEADS):
        cols = head_cols(head)
        values = beside_ones(value_ref[:, cols])
        for at in range(0, ROWS, CHUNK):
            end = at + CHUNK
            first = max(at - HALF, 0)
            mixed, top, total = absorb(
                q_ref[at:end, cols], key_ref[first:, cols], values[first:], bias_ref[at:end, first:],
                acc_ref[at:end, cols], top_ref[at:end, cols], total_ref[at:end, cols],
            )
            if at < HALF:
                acc2_ref[at:end, cols] = mixed
                top2_ref[at:end, cols] = top
                total2_ref[at:end, cols] = total
            else:
                context_ref[at - HALF : end - HALF, cols] = (mixed / total).astype(BF16)
    out = x_ref[:HALF].astype(F32) + dot(context_ref[...], wo_ref[...])
    out_ref[...] = out
    hid_ref[...] = out.astype(BF16)


def far_body(
    place_ref, xp_ref, wk_ref, wv_ref, wo_ref, x_ref, q_ref, acc_ref, top_ref, total_ref, seg_ref, marks_ref,
    out_ref, hid_ref, bias_ref, key_ref, value_ref, context_ref,
):
    segp, flagp = marks_of(place_ref, marks_ref, slice(0, HALF))
    row, col = square(HALF, HALF)
    same = same_user(seg_ref[:, :HALF], segp, flagp)
    bias_ref[...] = jnp.where(same & (col > row), 0.0, NEGATIVE)
    xp = xp_ref[...]
    key_ref[...] = dot(xp, wk_ref[...]).astype(BF16)
    value_ref[...] = dot(xp, wv_ref[...]).astype(BF16)
    for head in range(HEADS):
        cols = head_cols(head)
        values = beside_ones(value_ref[:, cols])
        for at in range(0, HALF, CHUNK):
            end = at + CHUNK
            mixed, top, total = absorb(
                q_ref[at:end, cols], key_ref[at:, cols], values[at:], bias_ref[at:end, at:],
                acc_ref[at:end, cols], top_ref[at:end, cols], total_ref[at:end, cols],
            )
            context_ref[at:end, cols] = (mixed / total).astype(BF16)
    out = x_ref[...].astype(F32) + dot(context_ref[...], wo_ref[...])
    out_ref[...] = out
    hid_ref[...] = out.astype(BF16)


def split_terms(stats, width):
    _, lane = square(*stats.shape)
    stats = jnp.where(lane < width, stats, 0.0)
    high = stats.astype(BF16).astype(F32)
    rest = stats - high
    middle = rest.astype(BF16).astype(F32)
    low = rest - middle
    return (high + pltpu.roll(middle, width, 1) + pltpu.roll(low, 2 * width, 1)).astype(BF16)


def join_terms(extra, width):
    extra = extra.astype(F32)
    return extra + pltpu.roll(extra, 128 - width, 1) + pltpu.roll(extra, 128 - 2 * width, 1)


def pool_body(
    place_ref, low_ref, high_ref, hid_low_ref, hid_high_ref, k_ref, sq_ref, uq_ref, seg_ref, marks_ref, flag_ref,
    keep_ref, send_ref, out_hbm, sems,
):
    writes = [
        pltpu.make_async_copy(low_ref, out_hbm.at[pl.ds(0, HALF)], sems.at[0]),
        pltpu.make_async_copy(high_ref, out_hbm.at[pl.ds(HALF, HALF)], sems.at[1]),
    ]
    for write in writes:
        write.start()
    core = place_ref[0]
    own_user = place_ref[1]
    count = USERS * SEEDS
    row, col = square(count, USERS)
    user16 = ((row % 32) // 4) * 2 + (core ^ (row // 128))
    seed16 = ((row % 128) // 32) * 4 + row % 4
    pick_seed = jnp.where(col == seed16, 1.0, 0.0).astype(BF16)
    apart = user16 ^ own_user
    place = (apart & 3) | ((apart & 4) << 1) | ((apart & 8) >> 1)
    pick_user = jnp.where(col == place, 1.0, 0.0).astype(BF16)
    seeds = dot(pick_seed, sq_ref[...]).astype(BF16)
    users = dot(pick_user, uq_ref[...]).astype(BF16)

    segs = seg_ref[...]
    segp, _ = marks_of(place_ref, marks_ref, slice(ROWS - 128, ROWS))
    lanes = lax.broadcasted_iota(jnp.int32, (8, ROWS), 1)
    before = pltpu.roll(jnp.broadcast_to(segs, (8, ROWS)), 1, 1)
    before = jnp.where(lanes == 0, segp[:, 127:], before)
    usable = (flag_ref[...] == 1) | (segs != before[0:1])
    marked = jnp.where(usable, segs, -1)
    wide, _ = square(count, ROWS)
    user_of = ((wide % 32) // 4) * 2 + (core ^ (wide // 128))
    bias = jnp.where(marked == user_of, 0.0, NEGATIVE)

    _, lane = square(count, 128)
    stats = jnp.zeros((count, 128), F32)
    for head in range(HEADS):
        cols = head_cols(head)
        keys = k_ref[:, cols]
        queries = jnp.concatenate([seeds[:, cols], users[:, cols]], 1)
        score = dot_rows(queries, jnp.concatenate([keys, keys], 1)) * SCALE + bias
        top = jnp.maximum(jnp.max(score, 1, keepdims=True), ABSENT)
        weight = jnp.exp2(score - top).astype(BF16)
        pooled = dot(weight[:, :HALF], beside_ones(hid_low_ref[:, cols]))
        pooled = pooled + dot(weight[:, HALF:], beside_ones(hid_high_ref[:, cols]))
        sums = pooled[:, :HEAD_DIM].astype(BF16)
        keep_ref[:, cols] = sums[:128]
        send_ref[:, cols] = sums[128:]
        stats = jnp.where(lane == head, top, jnp.where(lane == head + 8, pooled[:, HEAD_DIM:], stats))
    extra = split_terms(stats, 16)
    keep_ref[:, WIDTH:] = extra[:128]
    send_ref[:, WIDTH:] = extra[128:]
    for write in writes:
        write.wait()


def fold(left, right):
    left = left.reshape(16, 8, 128)
    right = right.reshape(16, 8, 128)
    upper = lax.broadcasted_iota(jnp.int32, left.shape, 1) < 4
    even = jnp.where(upper, left, pltpu.roll(right, 4, 1))
    odd = jnp.where(upper, pltpu.roll(left, 4, 1), right)
    return jnp.stack([even, odd], 1).reshape(256, 128)


def merge_body(a_ref, b_ref, out_ref):
    a = join_terms(a_ref[:, WIDTH:], 16)
    b = join_terms(b_ref[:, WIDTH:], 16)
    top = jnp.maximum(a, b)
    scale_a = jnp.exp2(a - top)
    scale_b = jnp.exp2(b - top)
    _, lane = square(*a.shape)
    total = a * pltpu.roll(scale_a, 8, 1) + b * pltpu.roll(scale_b, 8, 1)
    stats = jnp.where(lane < 8, top, total)
    ahead = pltpu.roll(stats, 124, 1)
    first = jnp.where(lane < 4, stats, ahead)
    second = jnp.where(lane < 4, ahead, pltpu.roll(stats, 120, 1))
    out_ref[:, SPAN:] = split_terms(fold(first, second), 8)

    def joined(head):
        cols = head_cols(head)
        return (
            a_ref[:, cols].astype(F32) * scale_a[:, head : head + 1]
            + b_ref[:, cols].astype(F32) * scale_b[:, head : head + 1]
        )

    for head in range(HEADS // 2):
        out_ref[:, head_cols(head)] = fold(joined(head), joined(head + HEADS // 2)).astype(BF16)


def finish_body(in_ref, comp_ref, row_ref):
    stats = join_terms(in_ref[:, SPAN:], 8).reshape(32, 8, 128)
    top = jnp.max(stats, 0)
    scale = jnp.exp2(stats - top[None])
    total = jnp.sum(stats * pltpu.roll(scale, 4, 2), 0)
    parts = []
    for head in range(HEADS // 2):
        data = in_ref[:, head_cols(head)].astype(F32).reshape(32, 8, 128)
        part = jnp.sum(data * scale[:, :, head : head + 1], 0)
        parts.append(part / total[:, head + 4 : head + 5])
    pooled = jnp.concatenate(parts, 1)
    power = jnp.broadcast_to(jnp.sum(pooled * pooled, 1, keepdims=True), (8, 128))
    power = power + pltpu.roll(power, 4, 0)
    scale = lax.rsqrt(power * (1.0 / WIDTH) + 1e-06)
    summary = (pooled * scale[:, :1]).astype(BF16)
    context = dot(summary, comp_ref[:SPAN]) + pltpu.roll(dot(summary, comp_ref[SPAN:]), 4, 0)
    row_ref[...] = context.astype(BF16).astype(F32)


def rank_body(row_ref, down_ref, rank_ref):
    context = row_ref[...].astype(BF16)
    rank = jnp.zeros((1, 128), F32)
    for seed in range(4):
        rank = rank + dot(context, down_ref[seed * 512 : (seed + 1) * 512, :])[seed : seed + 1]
    rank_ref[...] = jnp.broadcast_to(rank, (8, 128))


def cross_body(row_ref, a_ref, b_ref, c_ref, d_ref, up_ref, bias_ref, out_ref):
    rank = a_ref[0:1] + b_ref[0:1] + c_ref[0:1] + d_ref[0:1]
    rank = jnp.broadcast_to(rank, (8, 128)).astype(BF16)
    lifted = dot(rank, up_ref[...])[0:1]
    base = jnp.concatenate([row_ref[seed : seed + 1, :] for seed in range(4)], 1)
    out_ref[...] = base * (lifted + bias_ref[...].astype(F32)) + base


def shape(dims, dtype):
    return jax.ShapeDtypeStruct(dims, dtype)


VMEM = pl.BlockSpec(memory_space=pltpu.VMEM)
SMEM = pl.BlockSpec(memory_space=pltpu.SMEM)
HBM = pl.BlockSpec(memory_space=pltpu.HBM)


def call(name, body, outs, args, ins=None, scratch=(), out_specs=None, flops=1 << 28, nbytes=1 << 20, limit=16):
    return pl.pallas_call(
        body,
        in_specs=ins or [VMEM] * len(args),
        out_specs=out_specs or [VMEM] * len(outs),
        out_shape=outs,
        scratch_shapes=list(scratch),
        compiler_params=pltpu.CompilerParams(vmem_limit_bytes=limit << 20),
        cost_estimate=pl.CostEstimate(flops=1, bytes_accessed=1, transcendentals=0),
        name=name,
    )(*args)


def in_hbm(array):
    return pltpu.with_memory_space_constraint(array, pltpu.HBM)


def after(values, result):
    return lax.optimization_barrier((values, result))


def swap(value):
    return lax.ppermute(value, ("y", "x"), [(q * 4 + g, g * 4 + q) for q in range(4) for g in range(4)])


def turn(value, by):
    return lax.ppermute(value, "x", [(i, (i + by) % 4) for i in range(4)])


def first_rows(value):
    pairs = [
        (((x * 8 + z) * 4) + y, ((y * 8 + (z ^ (2 * y))) * 4) + x)
        for x in range(4) for y in range(4) for z in range(8)
    ]
    return lax.ppermute(value, ("y", "z", "x"), pairs)


def flip(value, axis, size, bit):
    return lax.ppermute(value, axis, [(i, i ^ bit) for i in range(size)])


def local(
    events, segment_ids, event_mask, nonseq, seed_tokens, w_query, w_key, w_value, w_out, w_pers,
    w_comp, w_down, w_up, cross_bias,
):
    x = events[0]
    first = (lax.axis_index("y") == 0) & (lax.axis_index("z") == 0) & (lax.axis_index("core") == 0)
    core = lax.axis_index("core").astype(jnp.int32)
    own_user = (lax.axis_index("z") ^ (2 * lax.axis_index("y"))).astype(jnp.int32) * 2 + core
    place = jnp.stack([core, own_user, first.astype(jnp.int32)])
    line = ("y", "z", "core")
    onward = [(i, i + 1) for i in range(63)]
    square_w = shape((WIDTH, WIDTH), BF16)
    rows_b = shape((ROWS, WIDTH), BF16)
    rows_f = shape((ROWS, WIDTH), F32)
    half_f = shape((HALF, WIDTH), F32)
    half_b = shape((HALF, WIDTH), BF16)
    line_i = shape((1, ROWS), jnp.int32)

    users = [first_rows(nonseq)]
    carried = shape((HALF + 16, WIDTH), BF16)
    high_x, low_x, segs, flags = call(
        "load", load_body, [carried, half_b] + [line_i] * 2, [in_hbm(a) for a in (x, segment_ids, event_mask)],
        [HBM] * 3, [pltpu.SemaphoreType.DMA((6,))],
    )
    near_x = lax.ppermute(high_x, line, onward)
    far_x = lax.ppermute(low_x, line, onward)

    w_query, w_key, w_value, w_out, q, k, v, bias = call(
        "project", project_body,
        [square_w] * 4 + [rows_b] * 3 + [shape((ROWS, ROWS), F32)],
        [place, low_x, high_x] + [in_hbm(a) for a in (w_query, w_key, w_value, w_out)] + [segs, flags],
        [SMEM] + [VMEM] * 2 + [HBM] * 4 + [VMEM] * 2,
        [pltpu.SemaphoreType.DMA((1 + 3 * WIDTH // PIECE,))],
        flops=3 << 30, nbytes=8 << 20, limit=16,
    )
    users, q = after(users, q)
    users.append(flip(users[0], "core", 2, 1))
    users.append(flip(jnp.concatenate(users, 0), "z", 8, 1))
    acc, top, total = call(
        "own", own_body, [rows_f] * 3, [q, k, v, bias], flops=2 << 30, nbytes=4 << 20, limit=16
    )
    users, acc = after(users, acc)
    users.append(flip(jnp.concatenate(users, 0), "y", 4, 2))

    scratch = [
        pltpu.VMEM((ROWS, HALF), F32), pltpu.VMEM((HALF, WIDTH), BF16), pltpu.VMEM((HALF, WIDTH), BF16),
        pltpu.VMEM((HALF, WIDTH), BF16),
    ]
    high, hid_high, acc, top, total = call(
        "near", near_body, [half_f, half_b] + [half_f] * 3,
        [place, near_x, w_key, w_value, w_out, high_x, q, acc, top, total, segs],
        [SMEM] + [VMEM] * 10, scratch, flops=3 << 30, nbytes=6 << 20,
    )
    users, top = after(users, top)
    users.append(flip(jnp.concatenate(users, 0), "y", 4, 1))
    low, hid_low = call(
        "far", far_body, [half_f, half_b],
        [place, far_x, w_key, w_value, w_out, low_x, q, acc, top, total, segs, near_x],
        [SMEM] + [VMEM] * 11, [pltpu.VMEM((HALF, HALF), F32)] + scratch[1:],
        flops=2 << 30, nbytes=4 << 20,
    )
    few = shape((SEEDS, WIDTH), BF16)
    seed_query, user_query = call("query", query_body, [few, few], users + [w_pers, w_query, seed_tokens])
    part = shape((128, MESSAGE), BF16)
    keep, send, out = call(
        "pool", pool_body, [part, part, rows_f],
        [place, low, high, hid_low, hid_high, k, seed_query, user_query, segs, near_x, flags],
        [SMEM] + [VMEM] * 10, [pltpu.SemaphoreType.DMA((2,))], [VMEM, VMEM, HBM],
        flops=1 << 30, nbytes=3 << 20,
    )
    merged = call(
        "merge", merge_body, [shape((256, SPAN + EXTRA), BF16)], [keep, flip(send, "core", 2, 1)]
    )[0]
    pieces = lax.all_to_all(merged.reshape(32, 8, SPAN + EXTRA), ("y", "z"), 0, 0, tiled=True)
    row = call(
        "finish", finish_body, [shape((8, 512), F32)], [pieces.reshape(256, SPAN + EXTRA), w_comp]
    )[0]
    row = swap(row)
    rank = call("rank", rank_body, [shape((8, 128), F32)], [row, w_down])[0]
    ranks = [rank] + [turn(rank, by) for by in (1, 2, 3)]
    cross = call("cross", cross_body, [shape((1, 2048), F32)], [row] + ranks + [w_up, cross_bias[None]])[0]
    return out[None], cross


def solution(mesh):
    split = Mesh(mesh.devices.reshape(4, 8, 2, 4), ("y", "z", "core", "x"))
    seq = ("y", "z", "core")
    return jax.shard_map(
        local,
        mesh=split,
        in_specs=(
            P("x", seq, None), P("x", seq), P("x", seq), P(seq, None),
            P(), P(), P(), P(), P(), P(), P(),
            P("x", None), P(None, "x"), P("x"),
        ),
        out_specs=(P("x", seq, None), P(seq, "x")),
        check_vma=False,
    )
```

```python
import functools
import jax
import jax.numpy as jnp
from jax import lax
from jax.experimental import pallas as pl
from jax.experimental.pallas import tpu as pltpu
from jax.sharding import Mesh, PartitionSpec as P

HEADS = 8
HEAD_DIM = 128
SEEDS = 16
USERS = 16
ROWS = 512
WIDTH = 1024
HALF = 256
PIECE = 512
EXTRA = 128
MESSAGE = WIDTH + EXTRA
SPAN = WIDTH // 2
NEGATIVE = -1e30
ABSENT = -1e29
LOG2E = 1.4426950408889634
SCALE = HEAD_DIM**-0.5 * LOG2E
F32 = jnp.float32
BF16 = jnp.bfloat16


def dot(a, b):
    return jnp.dot(a, b, preferred_element_type=F32)


def dot_rows(a, b):
    return lax.dot_general(a, b, (((1,), (1,)), ((), ())), preferred_element_type=F32)


def same_user(query_segments, key_segments, key_flags):
    def users(ids, kept):
        ones = (ids == lax.broadcasted_iota(jnp.int32, (USERS, ids.shape[1]), 0)) & kept
        return jnp.where(ones, 1.0, 0.0).astype(BF16)

    left = users(query_segments, True)
    right = users(key_segments, key_flags == 1)
    match = lax.dot_general(left, right, (((0,), (0,)), ((), ())), preferred_element_type=F32)
    return match > 0.5


def square(rows, cols):
    row = lax.broadcasted_iota(jnp.int32, (rows, cols), 0)
    return row, lax.broadcasted_iota(jnp.int32, (rows, cols), 1)


def head_cols(head):
    return slice(head * HEAD_DIM, (head + 1) * HEAD_DIM)


def beside_ones(values):
    return jnp.concatenate([values, jnp.ones(values.shape, BF16)], 1)


def load_body(x_hbm, seg_hbm, flag_hbm, x_ref, seg_ref, flag_ref, sems):
    quarter = ROWS // 4
    copies = [
        pltpu.make_async_copy(seg_hbm, seg_ref, sems.at[0]),
        pltpu.make_async_copy(flag_hbm, flag_ref, sems.at[1]),
    ]
    for at in range(0, ROWS, quarter):
        rows = pl.ds(at, quarter)
        copies.append(pltpu.make_async_copy(x_hbm.at[rows], x_ref.at[rows], sems.at[len(copies)]))
    for copy in copies:
        copy.start()
    copies[0].wait()
    copies[1].wait()
    row, _ = square(16, ROWS)
    marks = jnp.where(row == 0, seg_ref[...], jnp.where(row == 1, flag_ref[...], 0))
    x_ref[ROWS:, :ROWS] = marks.astype(F32).astype(BF16)
    x_ref[ROWS:, ROWS:] = jnp.zeros((16, WIDTH - ROWS), BF16)
    for copy in copies[2:]:
        copy.wait()


def project_body(place_ref, x_ref, *refs):
    count = len(refs) // 3
    copies = []
    for source, target in zip(refs[:count], refs[count : 2 * count]):
        for at in range(0, WIDTH, PIECE):
            cols = slice(at, at + PIECE)
            copies.append(
                pltpu.make_async_copy(source.at[:, cols], target.at[:, cols], refs[-1].at[len(copies)])
            )
    ahead = 3
    for copy in copies[:ahead]:
        copy.start()
    x = x_ref[:ROWS]
    at = 0
    for weight, result in zip(refs[count : 2 * count], refs[2 * count : 3 * count]):
        for start in range(0, WIDTH, PIECE):
            cols = slice(start, start + PIECE)
            copies[at].wait()
            if at + ahead < len(copies):
                copies[at + ahead].start()
            result[:, cols] = dot(x, weight[:, cols]).astype(BF16)
            at += 1


def project(place, x, *weights):
    count = len(weights)
    found = call(
        "project", project_body,
        [shape((WIDTH, WIDTH), BF16)] * count + [shape((ROWS, WIDTH), BF16)] * count,
        [place, x] + [in_hbm(weight) for weight in weights], [SMEM, VMEM] + [HBM] * count,
        [pltpu.SemaphoreType.DMA((count * WIDTH // PIECE,))],
    )
    return found[:count], found[count:]


def query_body(a_ref, b_ref, c_ref, d_ref, e_ref, pers_ref, wq_ref, seed_ref, sq_ref, uq_ref):
    rows = [ref[...].astype(F32) for ref in (a_ref, b_ref, c_ref, d_ref, e_ref)]
    profile = dot(jnp.concatenate(rows, 0).astype(BF16), pers_ref[...])
    both = jnp.concatenate([seed_ref[...].astype(F32), profile], 0).astype(BF16)
    queries = dot(both, wq_ref[...]).astype(BF16)
    sq_ref[...] = queries[:SEEDS]
    uq_ref[...] = queries[SEEDS:]


def marks_of(place_ref, near_ref, cols):
    marks = near_ref[ROWS:, cols].astype(F32).astype(jnp.int32)
    return jnp.where(place_ref[2] == 1, -1, marks[0:1]), marks[1:2]


def masked(segments, key_segments, key_flags, ahead):
    count = key_segments.shape[1]
    row, col = square(HALF, count)
    row = row + ahead
    same = same_user(segments, key_segments, key_flags)
    inside = (col < row) & (col > row - ROWS)
    return jnp.where((same & inside) | (col == row), 0.0, NEGATIVE)


def attend(queries, keys, values, bias):
    score = dot_rows(queries, keys) * SCALE + bias
    top = jnp.max(score, 1, keepdims=True)
    mixed = dot(jnp.exp2(score - top).astype(BF16), beside_ones(values))
    return (mixed[:, :HEAD_DIM] / mixed[:, HEAD_DIM:]).astype(BF16)


def near_body(
    place_ref, xp_ref, wk_ref, wv_ref, wo_hbm, x_ref, q_ref, k_ref, v_ref, seg_ref, flag_ref,
    out_ref, hid_ref, key_ref, value_ref, wo_ref, bias_ref, context_ref, sems,
):
    copy = pltpu.make_async_copy(wo_hbm, wo_ref, sems.at[0])
    copy.start()
    segp, flagp = marks_of(place_ref, xp_ref, slice(HALF, ROWS))
    segments = jnp.concatenate([segp, seg_ref[...]], 1)
    flags = jnp.concatenate([flagp, flag_ref[...]], 1)
    bias_ref[...] = masked(seg_ref[:, HALF:], segments, flags, ROWS)
    xp = xp_ref[HALF:ROWS]
    key_ref[...] = dot(xp, wk_ref[...]).astype(BF16)
    value_ref[...] = dot(xp, wv_ref[...]).astype(BF16)
    for head in range(HEADS):
        cols = head_cols(head)
        context_ref[:, cols] = attend(
            q_ref[HALF:, cols],
            jnp.concatenate([key_ref[:, cols], k_ref[:, cols]], 0),
            jnp.concatenate([value_ref[:, cols], v_ref[:, cols]], 0),
            bias_ref[...],
        )
    copy.wait()
    out = x_ref[HALF:ROWS].astype(F32) + dot(context_ref[...], wo_ref[...])
    out_ref[...] = out
    hid_ref[...] = out.astype(BF16)


def far_body(
    place_ref, xp_ref, wk_ref, wv_ref, wo_ref, x_ref, q_ref, k_ref, v_ref, keyp_ref, valuep_ref, seg_ref,
    flag_ref, out_ref, hid_ref, key_ref, value_ref, bias_ref, context_ref,
):
    segp, flagp = marks_of(place_ref, xp_ref, slice(0, ROWS))
    segments = jnp.concatenate([segp, seg_ref[:, :HALF]], 1)
    flags = jnp.concatenate([flagp, flag_ref[:, :HALF]], 1)
    bias_ref[...] = masked(seg_ref[:, :HALF], segments, flags, ROWS)
    xp = xp_ref[:HALF]
    key_ref[...] = dot(xp, wk_ref[...]).astype(BF16)
    value_ref[...] = dot(xp, wv_ref[...]).astype(BF16)
    for head in range(HEADS):
        cols = head_cols(head)
        context_ref[:, cols] = attend(
            q_ref[:HALF, cols],
            jnp.concatenate([key_ref[:, cols], keyp_ref[:, cols], k_ref[:HALF, cols]], 0),
            jnp.concatenate([value_ref[:, cols], valuep_ref[:, cols], v_ref[:HALF, cols]], 0),
            bias_ref[...],
        )
    out = x_ref[:HALF].astype(F32) + dot(context_ref[...], wo_ref[...])
    out_ref[...] = out
    hid_ref[...] = out.astype(BF16)


def split_terms(stats, width):
    _, lane = square(*stats.shape)
    stats = jnp.where(lane < width, stats, 0.0)
    high = stats.astype(BF16).astype(F32)
    rest = stats - high
    middle = rest.astype(BF16).astype(F32)
    low = rest - middle
    return (high + pltpu.roll(middle, width, 1) + pltpu.roll(low, 2 * width, 1)).astype(BF16)


def join_terms(extra, width):
    extra = extra.astype(F32)
    return extra + pltpu.roll(extra, 128 - width, 1) + pltpu.roll(extra, 128 - 2 * width, 1)


def pool_body(
    place_ref, low_ref, high_ref, hid_low_ref, hid_high_ref, k_ref, sq_ref, uq_ref, seg_ref, marks_ref, flag_ref,
    keep_ref, send_ref, out_hbm, sems,
):
    writes = [
        pltpu.make_async_copy(low_ref, out_hbm.at[pl.ds(0, HALF)], sems.at[0]),
        pltpu.make_async_copy(high_ref, out_hbm.at[pl.ds(HALF, HALF)], sems.at[1]),
    ]
    for write in writes:
        write.start()
    core = place_ref[0]
    own_user = place_ref[1]
    count = USERS * SEEDS
    row, col = square(count, USERS)
    user16 = ((row % 32) // 4) * 2 + (core ^ (row // 128))
    seed16 = ((row % 128) // 32) * 4 + row % 4
    pick_seed = jnp.where(col == seed16, 1.0, 0.0).astype(BF16)
    pick_user = jnp.where(col == (user16 ^ own_user), 1.0, 0.0).astype(BF16)
    seeds = dot(pick_seed, sq_ref[...]).astype(BF16)
    users = dot(pick_user, uq_ref[...]).astype(BF16)

    segs = seg_ref[...]
    segp, _ = marks_of(place_ref, marks_ref, slice(ROWS - 128, ROWS))
    lanes = lax.broadcasted_iota(jnp.int32, (8, ROWS), 1)
    before = pltpu.roll(jnp.broadcast_to(segs, (8, ROWS)), 1, 1)
    before = jnp.where(lanes == 0, segp[:, 127:], before)
    usable = (flag_ref[...] == 1) | (segs != before[0:1])
    marked = jnp.where(usable, segs, -1)
    wide, _ = square(count, ROWS)
    user_of = ((wide % 32) // 4) * 2 + (core ^ (wide // 128))
    bias = jnp.where(marked == user_of, 0.0, NEGATIVE)

    _, lane = square(count, 128)
    stats = jnp.zeros((count, 128), F32)
    for head in range(HEADS):
        cols = head_cols(head)
        keys = k_ref[:, cols]
        queries = jnp.concatenate([seeds[:, cols], users[:, cols]], 1)
        score = dot_rows(queries, jnp.concatenate([keys, keys], 1)) * SCALE + bias
        top = jnp.maximum(jnp.max(score, 1, keepdims=True), ABSENT)
        weight = jnp.exp2(score - top).astype(BF16)
        pooled = dot(weight[:, :HALF], beside_ones(hid_low_ref[:, cols]))
        pooled = pooled + dot(weight[:, HALF:], beside_ones(hid_high_ref[:, cols]))
        sums = pooled[:, :HEAD_DIM].astype(BF16)
        keep_ref[:, cols] = sums[:128]
        send_ref[:, cols] = sums[128:]
        stats = jnp.where(lane == head, top, jnp.where(lane == head + 8, pooled[:, HEAD_DIM:], stats))
    extra = split_terms(stats, 16)
    keep_ref[:, WIDTH:] = extra[:128]
    send_ref[:, WIDTH:] = extra[128:]
    for write in writes:
        write.wait()


def fold(left, right):
    left = left.reshape(16, 8, 128)
    right = right.reshape(16, 8, 128)
    upper = lax.broadcasted_iota(jnp.int32, left.shape, 1) < 4
    even = jnp.where(upper, left, pltpu.roll(right, 4, 1))
    odd = jnp.where(upper, pltpu.roll(left, 4, 1), right)
    return jnp.stack([even, odd], 1).reshape(256, 128)


def merge_body(a_ref, b_ref, out_ref):
    a = join_terms(a_ref[:, WIDTH:], 16)
    b = join_terms(b_ref[:, WIDTH:], 16)
    top = jnp.maximum(a, b)
    scale_a = jnp.exp2(a - top)
    scale_b = jnp.exp2(b - top)
    _, lane = square(*a.shape)
    total = a * pltpu.roll(scale_a, 8, 1) + b * pltpu.roll(scale_b, 8, 1)
    stats = jnp.where(lane < 8, top, total)
    ahead = pltpu.roll(stats, 124, 1)
    first = jnp.where(lane < 4, stats, ahead)
    second = jnp.where(lane < 4, ahead, pltpu.roll(stats, 120, 1))
    out_ref[:, SPAN:] = split_terms(fold(first, second), 8)

    def joined(head):
        cols = head_cols(head)
        return (
            a_ref[:, cols].astype(F32) * scale_a[:, head : head + 1]
            + b_ref[:, cols].astype(F32) * scale_b[:, head : head + 1]
        )

    for head in range(HEADS // 2):
        out_ref[:, head_cols(head)] = fold(joined(head), joined(head + HEADS // 2)).astype(BF16)


def finish_body(in_ref, comp_ref, row_ref):
    stats = join_terms(in_ref[:, SPAN:], 8).reshape(32, 8, 128)
    top = jnp.max(stats, 0)
    scale = jnp.exp2(stats - top[None])
    total = jnp.sum(stats * pltpu.roll(scale, 4, 2), 0)
    parts = []
    for head in range(HEADS // 2):
        data = in_ref[:, head_cols(head)].astype(F32).reshape(32, 8, 128)
        part = jnp.sum(data * scale[:, :, head : head + 1], 0)
        parts.append(part / total[:, head + 4 : head + 5])
    pooled = jnp.concatenate(parts, 1)
    power = jnp.broadcast_to(jnp.sum(pooled * pooled, 1, keepdims=True), (8, 128))
    power = power + pltpu.roll(power, 4, 0)
    scale = lax.rsqrt(power * (1.0 / WIDTH) + 1e-06)
    summary = (pooled * scale[:, :1]).astype(BF16)
    context = dot(summary, comp_ref[:SPAN]) + pltpu.roll(dot(summary, comp_ref[SPAN:]), 4, 0)
    row_ref[...] = context.astype(BF16).astype(F32)


def rank_body(row_ref, down_ref, rank_ref):
    context = row_ref[...].astype(BF16)
    rank = jnp.zeros((1, 128), F32)
    for seed in range(4):
        rank = rank + dot(context, down_ref[seed * 512 : (seed + 1) * 512, :])[seed : seed + 1]
    rank_ref[...] = jnp.broadcast_to(rank, (8, 128))


def cross_body(row_ref, a_ref, b_ref, c_ref, d_ref, up_ref, bias_ref, out_ref):
    rank = a_ref[0:1] + b_ref[0:1] + c_ref[0:1] + d_ref[0:1]
    rank = jnp.broadcast_to(rank, (8, 128)).astype(BF16)
    lifted = dot(rank, up_ref[...])[0:1]
    base = jnp.concatenate([row_ref[seed : seed + 1, :] for seed in range(4)], 1)
    out_ref[...] = base * (lifted + bias_ref[...].astype(F32)) + base


def shape(dims, dtype):
    return jax.ShapeDtypeStruct(dims, dtype)


VMEM = pl.BlockSpec(memory_space=pltpu.VMEM)
SMEM = pl.BlockSpec(memory_space=pltpu.SMEM)
HBM = pl.BlockSpec(memory_space=pltpu.HBM)


def call(name, body, outs, args, ins=None, scratch=(), out_specs=None, flops=1 << 28, nbytes=1 << 20, limit=16):
    return pl.pallas_call(
        body,
        in_specs=ins or [VMEM] * len(args),
        out_specs=out_specs or [VMEM] * len(outs),
        out_shape=outs,
        scratch_shapes=list(scratch),
        compiler_params=pltpu.CompilerParams(vmem_limit_bytes=limit << 20),
        cost_estimate=pl.CostEstimate(flops=1, bytes_accessed=1, transcendentals=0),
        name=name,
    )(*args)


def in_hbm(array):
    return pltpu.with_memory_space_constraint(array, pltpu.HBM)


def after(values, result):
    return lax.optimization_barrier((values, result))


def swap(value):
    return lax.ppermute(value, ("y", "x"), [(q * 4 + g, g * 4 + q) for q in range(4) for g in range(4)])


def turn(value, by):
    return lax.ppermute(value, "x", [(i, (i + by) % 4) for i in range(4)])


def flip(value, axis, size, bit):
    return lax.ppermute(value, axis, [(i, i ^ bit) for i in range(size)])


def local(
    events, segment_ids, event_mask, nonseq, seed_tokens, w_query, w_key, w_value, w_out, w_pers,
    w_comp, w_down, w_up, cross_bias,
):
    x = events[0]
    first = (lax.axis_index("y") == 0) & (lax.axis_index("z") == 0) & (lax.axis_index("core") == 0)
    core = lax.axis_index("core").astype(jnp.int32)
    own_user = lax.axis_index("z").astype(jnp.int32) * 2 + core
    place = jnp.stack([core, own_user, first.astype(jnp.int32)])
    line = ("y", "z", "core")
    onward = [(i, i + 1) for i in range(63)]
    square_w = shape((WIDTH, WIDTH), BF16)
    rows_b = shape((ROWS, WIDTH), BF16)
    rows_f = shape((ROWS, WIDTH), F32)
    half_f = shape((HALF, WIDTH), F32)
    half_b = shape((HALF, WIDTH), BF16)
    line_i = shape((1, ROWS), jnp.int32)

    users = [swap(nonseq)]
    x, segs, flags = call(
        "load", load_body, [shape((ROWS + 16, WIDTH), BF16)] + [line_i] * 2,
        [in_hbm(a) for a in (x, segment_ids, event_mask)], [HBM] * 3, [pltpu.SemaphoreType.DMA((6,))],
    )
    prior = lax.ppermute(x, line, onward)

    (w_query, w_key), (q, k) = project(place, x, w_query, w_key)
    users, q = after(users, q)
    users.append(flip(users[0], "core", 2, 1))
    users, x = after(users, x)
    users.append(flip(jnp.concatenate(users, 0), "z", 8, 1))
    (w_value,), (v,) = project(place, x, w_value)
    users, v = after(users, v)
    users.append(flip(jnp.concatenate(users, 0), "z", 8, 2))
    scratch = [pltpu.VMEM((HALF, HALF + ROWS), F32), pltpu.VMEM((HALF, WIDTH), BF16)]
    high, hid_high, near_k, near_v, w_out = call(
        "near", near_body, [half_f] + [half_b] * 3 + [square_w],
        [place, prior, w_key, w_value, in_hbm(w_out), x, q, k, v, segs, flags],
        [SMEM] + [VMEM] * 3 + [HBM] + [VMEM] * 6, scratch + [pltpu.SemaphoreType.DMA((1,))],
    )
    users, near_k = after(users, near_k)
    users.append(flip(jnp.concatenate(users, 0), "z", 8, 4))
    low, hid_low = call(
        "far", far_body, [half_f, half_b],
        [place, prior, w_key, w_value, w_out, x, q, k, v, near_k, near_v, segs, flags],
        [SMEM] + [VMEM] * 12, [pltpu.VMEM((HALF, WIDTH), BF16)] * 2 + scratch,
    )
    few = shape((SEEDS, WIDTH), BF16)
    seed_query, user_query = call("query", query_body, [few, few], users + [w_pers, w_query, seed_tokens])
    part = shape((128, MESSAGE), BF16)
    keep, send, out = call(
        "pool", pool_body, [part, part, rows_f],
        [place, low, high, hid_low, hid_high, k, seed_query, user_query, segs, prior, flags],
        [SMEM] + [VMEM] * 10, [pltpu.SemaphoreType.DMA((2,))], [VMEM, VMEM, HBM],
        flops=1 << 30, nbytes=3 << 20,
    )
    merged = call(
        "merge", merge_body, [shape((256, SPAN + EXTRA), BF16)], [keep, flip(send, "core", 2, 1)]
    )[0]
    pieces = lax.all_to_all(merged.reshape(32, 8, SPAN + EXTRA), ("y", "z"), 0, 0, tiled=True)
    row = call(
        "finish", finish_body, [shape((8, 512), F32)], [pieces.reshape(256, SPAN + EXTRA), w_comp]
    )[0]
    row = swap(row)
    rank = call("rank", rank_body, [shape((8, 128), F32)], [row, w_down])[0]
    ranks = [rank] + [turn(rank, by) for by in (1, 2, 3)]
    cross = call("cross", cross_body, [shape((1, 2048), F32)], [row] + ranks + [w_up, cross_bias[None]])[0]
    return out[None], cross


def solution(mesh):
    split = Mesh(mesh.devices.reshape(4, 8, 2, 4), ("y", "z", "core", "x"))
    seq = ("y", "z", "core")
    return jax.shard_map(
        local,
        mesh=split,
        in_specs=(
            P("x", seq, None), P("x", seq), P("x", seq), P(seq, None),
            P(), P(), P(), P(), P(), P(), P(),
            P("x", None), P(None, "x"), P("x"),
        ),
        out_specs=(P("x", seq, None), P(seq, "x")),
        check_vma=False,
    )
```

```python
import functools
import jax
import jax.numpy as jnp
from jax import lax
from jax.experimental import pallas as pl
from jax.experimental.pallas import tpu as pltpu
from jax.sharding import Mesh, PartitionSpec as P

HEADS = 8
HEAD_DIM = 128
SEEDS = 16
USERS = 16
ROWS = 512
WIDTH = 1024
HALF = 256
CHUNK = 128
PIECE = 512
EXTRA = 128
MESSAGE = WIDTH + EXTRA
SPAN = WIDTH // 2
NEGATIVE = -1e30
ABSENT = -1e29
LOG2E = 1.4426950408889634
SCALE = HEAD_DIM**-0.5 * LOG2E
F32 = jnp.float32
BF16 = jnp.bfloat16


def dot(a, b):
    return jnp.dot(a, b, preferred_element_type=F32)


def dot_rows(a, b):
    return lax.dot_general(a, b, (((1,), (1,)), ((), ())), preferred_element_type=F32)


def same_user(query_segments, key_segments, key_flags):
    def users(ids, kept):
        ones = (ids == lax.broadcasted_iota(jnp.int32, (USERS, ids.shape[1]), 0)) & kept
        return jnp.where(ones, 1.0, 0.0).astype(BF16)

    left = users(query_segments, True)
    right = users(key_segments, key_flags == 1)
    match = lax.dot_general(left, right, (((0,), (0,)), ((), ())), preferred_element_type=F32)
    return match > 0.5


def square(rows, cols):
    row = lax.broadcasted_iota(jnp.int32, (rows, cols), 0)
    return row, lax.broadcasted_iota(jnp.int32, (rows, cols), 1)


def head_cols(head):
    return slice(head * HEAD_DIM, (head + 1) * HEAD_DIM)


def beside_ones(values):
    return jnp.concatenate([values, jnp.ones(values.shape, BF16)], 1)


def load_body(x_hbm, seg_hbm, flag_hbm, x_ref, seg_ref, flag_ref, sems):
    quarter = ROWS // 4
    copies = [
        pltpu.make_async_copy(seg_hbm, seg_ref, sems.at[0]),
        pltpu.make_async_copy(flag_hbm, flag_ref, sems.at[1]),
    ]
    for at in range(0, ROWS, quarter):
        rows = pl.ds(at, quarter)
        copies.append(pltpu.make_async_copy(x_hbm.at[rows], x_ref.at[rows], sems.at[len(copies)]))
    for copy in copies:
        copy.start()
    copies[0].wait()
    copies[1].wait()
    row, _ = square(16, ROWS)
    marks = jnp.where(row == 0, seg_ref[...], jnp.where(row == 1, flag_ref[...], 0))
    x_ref[ROWS:, :ROWS] = marks.astype(F32).astype(BF16)
    x_ref[ROWS:, ROWS:] = jnp.zeros((16, WIDTH - ROWS), BF16)
    for copy in copies[2:]:
        copy.wait()


def project_body(place_ref, x_ref, *refs):
    count = len(refs) // 3
    copies = []
    for source, target in zip(refs[:count], refs[count : 2 * count]):
        for at in range(0, WIDTH, PIECE):
            cols = slice(at, at + PIECE)
            copies.append(
                pltpu.make_async_copy(source.at[:, cols], target.at[:, cols], refs[-1].at[len(copies)])
            )
    ahead = 3
    for copy in copies[:ahead]:
        copy.start()
    x = x_ref[:ROWS]
    at = 0
    for weight, result in zip(refs[count : 2 * count], refs[2 * count : 3 * count]):
        for start in range(0, WIDTH, PIECE):
            cols = slice(start, start + PIECE)
            copies[at].wait()
            if at + ahead < len(copies):
                copies[at + ahead].start()
            result[:, cols] = dot(x, weight[:, cols]).astype(BF16)
            at += 1


def project(place, x, *weights):
    count = len(weights)
    found = call(
        "project", project_body,
        [shape((WIDTH, WIDTH), BF16)] * count + [shape((ROWS, WIDTH), BF16)] * count,
        [place, x] + [in_hbm(weight) for weight in weights], [SMEM, VMEM] + [HBM] * count,
        [pltpu.SemaphoreType.DMA((count * WIDTH // PIECE,))],
    )
    return found[:count], found[count:]


def query_body(a_ref, b_ref, c_ref, d_ref, e_ref, pers_ref, wq_ref, seed_ref, sq_ref, uq_ref):
    rows = [ref[...].astype(F32) for ref in (a_ref, b_ref, c_ref, d_ref, e_ref)]
    profile = dot(jnp.concatenate(rows, 0).astype(BF16), pers_ref[...])
    both = jnp.concatenate([seed_ref[...].astype(F32), profile], 0).astype(BF16)
    queries = dot(both, wq_ref[...]).astype(BF16)
    sq_ref[...] = queries[:SEEDS]
    uq_ref[...] = queries[SEEDS:]


def marks_of(place_ref, near_ref, cols):
    marks = near_ref[ROWS:, cols].astype(F32).astype(jnp.int32)
    return jnp.where(place_ref[2] == 1, -1, marks[0:1]), marks[1:2]


def masked(segments, key_segments, key_flags, ahead):
    count = key_segments.shape[1]
    row, col = square(HALF, count)
    row = row + ahead
    same = same_user(segments, key_segments, key_flags)
    inside = (col < row) & (col > row - ROWS)
    return jnp.where((same & inside) | (col == row), 0.0, NEGATIVE)


def attend(queries, keys, values, bias):
    score = dot_rows(queries, keys) * SCALE + bias
    top = jnp.max(score, 1, keepdims=True)
    mixed = dot(jnp.exp2(score - top).astype(BF16), beside_ones(values))
    return (mixed[:, :HEAD_DIM] / mixed[:, HEAD_DIM:]).astype(BF16)


def near_body(
    place_ref, xp_ref, wk_ref, wv_ref, wo_hbm, x_ref, q_ref, k_ref, v_ref, seg_ref, flag_ref,
    out_ref, hid_ref, key_ref, value_ref, wo_ref, bias_ref, context_ref, sems,
):
    copy = pltpu.make_async_copy(wo_hbm, wo_ref, sems.at[0])
    copy.start()
    segp, flagp = marks_of(place_ref, xp_ref, slice(HALF, ROWS))
    segments = jnp.concatenate([segp, seg_ref[...]], 1)
    flags = jnp.concatenate([flagp, flag_ref[...]], 1)
    bias_ref[...] = masked(seg_ref[:, HALF:], segments, flags, ROWS)
    xp = xp_ref[HALF:ROWS]
    key_ref[...] = dot(xp, wk_ref[...]).astype(BF16)
    value_ref[...] = dot(xp, wv_ref[...]).astype(BF16)
    for head in range(HEADS):
        cols = head_cols(head)
        keys = jnp.concatenate([key_ref[:, cols], k_ref[:, cols]], 0)
        values = jnp.concatenate([value_ref[:, cols], v_ref[:, cols]], 0)
        for at in range(0, HALF, CHUNK):
            end = at + CHUNK
            context_ref[at:end, cols] = attend(
                q_ref[HALF + at : HALF + end, cols], keys[at : end + ROWS], values[at : end + ROWS],
                bias_ref[at:end, at : end + ROWS],
            )
    copy.wait()
    out = x_ref[HALF:ROWS].astype(F32) + dot(context_ref[...], wo_ref[...])
    out_ref[...] = out
    hid_ref[...] = out.astype(BF16)


def far_body(
    place_ref, xp_ref, wk_ref, wv_ref, wo_ref, x_ref, q_ref, k_ref, v_ref, keyp_ref, valuep_ref, seg_ref,
    flag_ref, out_ref, hid_ref, key_ref, value_ref, bias_ref, context_ref,
):
    segp, flagp = marks_of(place_ref, xp_ref, slice(0, ROWS))
    segments = jnp.concatenate([segp, seg_ref[:, :HALF]], 1)
    flags = jnp.concatenate([flagp, flag_ref[:, :HALF]], 1)
    bias_ref[...] = masked(seg_ref[:, :HALF], segments, flags, ROWS)
    xp = xp_ref[:HALF]
    key_ref[...] = dot(xp, wk_ref[...]).astype(BF16)
    value_ref[...] = dot(xp, wv_ref[...]).astype(BF16)
    for head in range(HEADS):
        cols = head_cols(head)
        keys = jnp.concatenate([key_ref[:, cols], keyp_ref[:, cols], k_ref[:HALF, cols]], 0)
        values = jnp.concatenate([value_ref[:, cols], valuep_ref[:, cols], v_ref[:HALF, cols]], 0)
        for at in range(0, HALF, CHUNK):
            end = at + CHUNK
            context_ref[at:end, cols] = attend(
                q_ref[at : end, cols], keys[at : end + ROWS], values[at : end + ROWS],
                bias_ref[at:end, at : end + ROWS],
            )
    out = x_ref[:HALF].astype(F32) + dot(context_ref[...], wo_ref[...])
    out_ref[...] = out
    hid_ref[...] = out.astype(BF16)


def split_terms(stats, width):
    _, lane = square(*stats.shape)
    stats = jnp.where(lane < width, stats, 0.0)
    high = stats.astype(BF16).astype(F32)
    rest = stats - high
    middle = rest.astype(BF16).astype(F32)
    low = rest - middle
    return (high + pltpu.roll(middle, width, 1) + pltpu.roll(low, 2 * width, 1)).astype(BF16)


def join_terms(extra, width):
    extra = extra.astype(F32)
    return extra + pltpu.roll(extra, 128 - width, 1) + pltpu.roll(extra, 128 - 2 * width, 1)


def pool_body(
    place_ref, low_ref, high_ref, hid_low_ref, hid_high_ref, k_ref, sq_ref, uq_ref, seg_ref, marks_ref, flag_ref,
    keep_ref, send_ref, out_hbm, sems,
):
    writes = [
        pltpu.make_async_copy(low_ref, out_hbm.at[pl.ds(0, HALF)], sems.at[0]),
        pltpu.make_async_copy(high_ref, out_hbm.at[pl.ds(HALF, HALF)], sems.at[1]),
    ]
    for write in writes:
        write.start()
    core = place_ref[0]
    own_user = place_ref[1]
    count = USERS * SEEDS
    row, col = square(count, USERS)
    user16 = ((row % 32) // 4) * 2 + (core ^ (row // 128))
    seed16 = ((row % 128) // 32) * 4 + row % 4
    pick_seed = jnp.where(col == seed16, 1.0, 0.0).astype(BF16)
    pick_user = jnp.where(col == (user16 ^ own_user), 1.0, 0.0).astype(BF16)
    seeds = dot(pick_seed, sq_ref[...]).astype(BF16)
    users = dot(pick_user, uq_ref[...]).astype(BF16)

    segs = seg_ref[...]
    segp, _ = marks_of(place_ref, marks_ref, slice(ROWS - 128, ROWS))
    lanes = lax.broadcasted_iota(jnp.int32, (8, ROWS), 1)
    before = pltpu.roll(jnp.broadcast_to(segs, (8, ROWS)), 1, 1)
    before = jnp.where(lanes == 0, segp[:, 127:], before)
    usable = (flag_ref[...] == 1) | (segs != before[0:1])
    marked = jnp.where(usable, segs, -1)
    wide, _ = square(count, ROWS)
    user_of = ((wide % 32) // 4) * 2 + (core ^ (wide // 128))
    bias = jnp.where(marked == user_of, 0.0, NEGATIVE)

    _, lane = square(count, 128)
    stats = jnp.zeros((count, 128), F32)
    for head in range(HEADS):
        cols = head_cols(head)
        keys = k_ref[:, cols]
        queries = jnp.concatenate([seeds[:, cols], users[:, cols]], 1)
        score = dot_rows(queries, jnp.concatenate([keys, keys], 1)) * SCALE + bias
        top = jnp.maximum(jnp.max(score, 1, keepdims=True), ABSENT)
        weight = jnp.exp2(score - top).astype(BF16)
        pooled = dot(weight[:, :HALF], beside_ones(hid_low_ref[:, cols]))
        pooled = pooled + dot(weight[:, HALF:], beside_ones(hid_high_ref[:, cols]))
        sums = pooled[:, :HEAD_DIM].astype(BF16)
        keep_ref[:, cols] = sums[:128]
        send_ref[:, cols] = sums[128:]
        stats = jnp.where(lane == head, top, jnp.where(lane == head + 8, pooled[:, HEAD_DIM:], stats))
    extra = split_terms(stats, 16)
    keep_ref[:, WIDTH:] = extra[:128]
    send_ref[:, WIDTH:] = extra[128:]
    for write in writes:
        write.wait()


def fold(left, right):
    left = left.reshape(16, 8, 128)
    right = right.reshape(16, 8, 128)
    upper = lax.broadcasted_iota(jnp.int32, left.shape, 1) < 4
    even = jnp.where(upper, left, pltpu.roll(right, 4, 1))
    odd = jnp.where(upper, pltpu.roll(left, 4, 1), right)
    return jnp.stack([even, odd], 1).reshape(256, 128)


def merge_body(a_ref, b_ref, out_ref):
    a = join_terms(a_ref[:, WIDTH:], 16)
    b = join_terms(b_ref[:, WIDTH:], 16)
    top = jnp.maximum(a, b)
    scale_a = jnp.exp2(a - top)
    scale_b = jnp.exp2(b - top)
    _, lane = square(*a.shape)
    total = a * pltpu.roll(scale_a, 8, 1) + b * pltpu.roll(scale_b, 8, 1)
    stats = jnp.where(lane < 8, top, total)
    ahead = pltpu.roll(stats, 124, 1)
    first = jnp.where(lane < 4, stats, ahead)
    second = jnp.where(lane < 4, ahead, pltpu.roll(stats, 120, 1))
    out_ref[:, SPAN:] = split_terms(fold(first, second), 8)

    def joined(head):
        cols = head_cols(head)
        return (
            a_ref[:, cols].astype(F32) * scale_a[:, head : head + 1]
            + b_ref[:, cols].astype(F32) * scale_b[:, head : head + 1]
        )

    for head in range(HEADS // 2):
        out_ref[:, head_cols(head)] = fold(joined(head), joined(head + HEADS // 2)).astype(BF16)


def finish_body(in_ref, comp_ref, row_ref):
    stats = join_terms(in_ref[:, SPAN:], 8).reshape(32, 8, 128)
    top = jnp.max(stats, 0)
    scale = jnp.exp2(stats - top[None])
    total = jnp.sum(stats * pltpu.roll(scale, 4, 2), 0)
    parts = []
    for head in range(HEADS // 2):
        data = in_ref[:, head_cols(head)].astype(F32).reshape(32, 8, 128)
        part = jnp.sum(data * scale[:, :, head : head + 1], 0)
        parts.append(part / total[:, head + 4 : head + 5])
    pooled = jnp.concatenate(parts, 1)
    power = jnp.broadcast_to(jnp.sum(pooled * pooled, 1, keepdims=True), (8, 128))
    power = power + pltpu.roll(power, 4, 0)
    scale = lax.rsqrt(power * (1.0 / WIDTH) + 1e-06)
    summary = (pooled * scale[:, :1]).astype(BF16)
    context = dot(summary, comp_ref[:SPAN]) + pltpu.roll(dot(summary, comp_ref[SPAN:]), 4, 0)
    row_ref[...] = context.astype(BF16).astype(F32)


def rank_body(row_ref, down_ref, rank_ref):
    context = row_ref[...].astype(BF16)
    rank = jnp.zeros((1, 128), F32)
    for seed in range(4):
        rank = rank + dot(context, down_ref[seed * 512 : (seed + 1) * 512, :])[seed : seed + 1]
    rank_ref[...] = jnp.broadcast_to(rank, (8, 128))


def cross_body(row_ref, a_ref, b_ref, c_ref, d_ref, up_ref, bias_ref, out_ref):
    rank = a_ref[0:1] + b_ref[0:1] + c_ref[0:1] + d_ref[0:1]
    rank = jnp.broadcast_to(rank, (8, 128)).astype(BF16)
    lifted = dot(rank, up_ref[...])[0:1]
    base = jnp.concatenate([row_ref[seed : seed + 1, :] for seed in range(4)], 1)
    out_ref[...] = base * (lifted + bias_ref[...].astype(F32)) + base


def shape(dims, dtype):
    return jax.ShapeDtypeStruct(dims, dtype)


VMEM = pl.BlockSpec(memory_space=pltpu.VMEM)
SMEM = pl.BlockSpec(memory_space=pltpu.SMEM)
HBM = pl.BlockSpec(memory_space=pltpu.HBM)


def call(name, body, outs, args, ins=None, scratch=(), out_specs=None, flops=1 << 28, nbytes=1 << 20, limit=16):
    return pl.pallas_call(
        body,
        in_specs=ins or [VMEM] * len(args),
        out_specs=out_specs or [VMEM] * len(outs),
        out_shape=outs,
        scratch_shapes=list(scratch),
        compiler_params=pltpu.CompilerParams(vmem_limit_bytes=limit << 20),
        cost_estimate=pl.CostEstimate(flops=1, bytes_accessed=1, transcendentals=0),
        name=name,
    )(*args)


def in_hbm(array):
    return pltpu.with_memory_space_constraint(array, pltpu.HBM)


def after(values, result):
    return lax.optimization_barrier((values, result))


def swap(value):
    return lax.ppermute(value, ("y", "x"), [(q * 4 + g, g * 4 + q) for q in range(4) for g in range(4)])


def turn(value, by):
    return lax.ppermute(value, "x", [(i, (i + by) % 4) for i in range(4)])


def flip(value, axis, size, bit):
    return lax.ppermute(value, axis, [(i, i ^ bit) for i in range(size)])


def local(
    events, segment_ids, event_mask, nonseq, seed_tokens, w_query, w_key, w_value, w_out, w_pers,
    w_comp, w_down, w_up, cross_bias,
):
    x = events[0]
    first = (lax.axis_index("y") == 0) & (lax.axis_index("z") == 0) & (lax.axis_index("core") == 0)
    core = lax.axis_index("core").astype(jnp.int32)
    own_user = lax.axis_index("z").astype(jnp.int32) * 2 + core
    place = jnp.stack([core, own_user, first.astype(jnp.int32)])
    line = ("y", "z", "core")
    onward = [(i, i + 1) for i in range(63)]
    square_w = shape((WIDTH, WIDTH), BF16)
    rows_b = shape((ROWS, WIDTH), BF16)
    rows_f = shape((ROWS, WIDTH), F32)
    half_f = shape((HALF, WIDTH), F32)
    half_b = shape((HALF, WIDTH), BF16)
    line_i = shape((1, ROWS), jnp.int32)

    users = [swap(nonseq)]
    x, segs, flags = call(
        "load", load_body, [shape((ROWS + 16, WIDTH), BF16)] + [line_i] * 2,
        [in_hbm(a) for a in (x, segment_ids, event_mask)], [HBM] * 3, [pltpu.SemaphoreType.DMA((6,))],
    )
    prior = lax.ppermute(x, line, onward)

    (w_query, w_key), (q, k) = project(place, x, w_query, w_key)
    users, q = after(users, q)
    users.append(flip(users[0], "core", 2, 1))
    users, x = after(users, x)
    users.append(flip(jnp.concatenate(users, 0), "z", 8, 1))
    (w_value,), (v,) = project(place, x, w_value)
    users, v = after(users, v)
    users.append(flip(jnp.concatenate(users, 0), "z", 8, 2))
    scratch = [pltpu.VMEM((HALF, HALF + ROWS), F32), pltpu.VMEM((HALF, WIDTH), BF16)]
    high, hid_high, near_k, near_v, w_out = call(
        "near", near_body, [half_f] + [half_b] * 3 + [square_w],
        [place, prior, w_key, w_value, in_hbm(w_out), x, q, k, v, segs, flags],
        [SMEM] + [VMEM] * 3 + [HBM] + [VMEM] * 6, scratch + [pltpu.SemaphoreType.DMA((1,))],
    )
    users, near_k = after(users, near_k)
    users.append(flip(jnp.concatenate(users, 0), "z", 8, 4))
    low, hid_low = call(
        "far", far_body, [half_f, half_b],
        [place, prior, w_key, w_value, w_out, x, q, k, v, near_k, near_v, segs, flags],
        [SMEM] + [VMEM] * 12, [pltpu.VMEM((HALF, WIDTH), BF16)] * 2 + scratch,
    )
    few = shape((SEEDS, WIDTH), BF16)
    seed_query, user_query = call("query", query_body, [few, few], users + [w_pers, w_query, seed_tokens])
    part = shape((128, MESSAGE), BF16)
    keep, send, out = call(
        "pool", pool_body, [part, part, rows_f],
        [place, low, high, hid_low, hid_high, k, seed_query, user_query, segs, prior, flags],
        [SMEM] + [VMEM] * 10, [pltpu.SemaphoreType.DMA((2,))], [VMEM, VMEM, HBM],
        flops=1 << 30, nbytes=3 << 20,
    )
    merged = call(
        "merge", merge_body, [shape((256, SPAN + EXTRA), BF16)], [keep, flip(send, "core", 2, 1)]
    )[0]
    pieces = lax.all_to_all(merged.reshape(32, 8, SPAN + EXTRA), ("y", "z"), 0, 0, tiled=True)
    row = call(
        "finish", finish_body, [shape((8, 512), F32)], [pieces.reshape(256, SPAN + EXTRA), w_comp]
    )[0]
    row = swap(row)
    rank = call("rank", rank_body, [shape((8, 128), F32)], [row, w_down])[0]
    ranks = [rank] + [turn(rank, by) for by in (1, 2, 3)]
    cross = call("cross", cross_body, [shape((1, 2048), F32)], [row] + ranks + [w_up, cross_bias[None]])[0]
    return out[None], cross


def solution(mesh):
    split = Mesh(mesh.devices.reshape(4, 8, 2, 4), ("y", "z", "core", "x"))
    seq = ("y", "z", "core")
    return jax.shard_map(
        local,
        mesh=split,
        in_specs=(
            P("x", seq, None), P("x", seq), P("x", seq), P(seq, None),
            P(), P(), P(), P(), P(), P(), P(),
            P("x", None), P(None, "x"), P("x"),
        ),
        out_specs=(P("x", seq, None), P(seq, "x")),
        check_vma=False,
    )
```
